512 devices in a mesh: section: 16 (over z), dp: 32 (over x, y, core).
Axes of the slice: x: 4, y: 4, z: 16, core: 2. Of those that a mesh axis runs over, the one named last changes fastest.
Arguments:
- saved_inputs: bfloat16 [16, 2, 2048, 4096], P('section', None, 'dp'), may hold values from -6 to 6
- loss_grad: bfloat16 [2, 2048, 4096], P(None, 'dp'), may hold values from -6 to 6
- w_in: bfloat16 [16, 4096, 128], P('section'), may hold values from -0.09375 to 0.09375
- w_out: bfloat16 [16, 128, 4096], P('section'), may hold values from -0.5 to 0.5
- left_root: bfloat16 [16, 32, 4, 128, 128], P('section', 'dp'), as said below
- right_root: bfloat16 [16, 32, 4, 128, 128], P('section', 'dp'), as said below
- momentum: float32 [16, 32, 4, 128, 128], P('section', 'dp'), may hold values from -6 to 6
- owned_blocks: int32 [16, 32, 4], P('section'), may hold values from 0 to 63, as said below
- owned_count: int32 [16, 32], P('section'), may hold values from 0 to 4, as said below
Outputs:
- new_momentum: float32 [16, 32, 4, 128, 128], P('section', 'dp')
- search_in: bfloat16 [16, 4096, 128], P('section', 'dp')
- search_out: bfloat16 [16, 128, 4096], P('section', None, 'dp')
The draws below stay inside these ranges and needn't reach their ends.
Inputs may be any that keep to these rules, and one draw needn't show every extreme that they name: `owned_blocks`: in each section every block id of 0 to 63 stands in exactly one owner's first owned_count slots; slots at or past the count hold 0. `owned_count`: sums to 64 over the owners of a section; some owner of every section holds 4 blocks. `left_root`: Symmetric. `right_root`: Symmetric.
All inputs are finite; a program needn't handle non-finite values.
Results may differ from the reference program's by a relative error of at most 0.035.
Values may be sent and summed in bfloat16 or wider, within the bound.
A program may use at most 64 MiB of HBM per device.

```python
import jax
import jax.numpy as jnp
from jax import lax

D = 4096
BLK = 128
TOK = 64
MB = 2
SECTIONS = 16
OWNERS = 32
TOKENS = 2048
NBLK = 64
CAP = 4


def root_matrices(key, lowest, highest):
    key_diag, key_noise = jax.random.split(key)
    shape = (SECTIONS, OWNERS, CAP, BLK, BLK)
    diagonal = jnp.exp(jax.random.uniform(key_diag, shape[:-1], jnp.float32, jnp.log(lowest), jnp.log(highest)))
    noise = jax.random.normal(key_noise, shape, jnp.float32) * (0.25 / jnp.sqrt(jnp.float32(BLK)))
    symmetric = (noise + jnp.swapaxes(noise, -1, -2)) * 0.7071067811865476
    return symmetric + diagonal[..., None] * jnp.eye(BLK, dtype=jnp.float32)


def section_assignment(key):
    key_blocks, key_owners, key_moves = jax.random.split(key, 3)
    middle = NBLK // OWNERS
    order_blocks = jax.random.permutation(key_blocks, NBLK).astype(jnp.int32)
    order_owners = jax.random.permutation(key_owners, OWNERS).astype(jnp.int32)
    moves = jax.random.randint(key_moves, (OWNERS // 2,), -middle, middle + 1).astype(jnp.int32)
    moves = moves.at[0].set(middle)
    paired = jnp.stack([middle + moves, middle - moves], axis=1).reshape(OWNERS)
    counts = jnp.zeros((OWNERS,), jnp.int32).at[order_owners].set(paired)
    starts = jnp.cumsum(counts) - counts
    slots = jnp.arange(CAP, dtype=jnp.int32)
    position = jnp.clip(starts[:, None] + slots[None, :], 0, NBLK - 1)
    live = slots[None, :] < counts[:, None]
    lists = jnp.where(live, order_blocks[position], 0).astype(jnp.int32)
    return (lists, counts)


def assignment(key):
    keys = jax.random.split(key, SECTIONS)
    return jax.vmap(section_assignment)(keys)


def draw_owned_blocks(key, part):
    return assignment(key)[0]


def draw_owned_count(key, part):
    return assignment(key)[1]


def draw_left_root(key, part):
    key = jax.random.fold_in(key, 11)
    return root_matrices(key, 0.6, 1.6).astype(jnp.bfloat16)


def draw_right_root(key, part):
    key = jax.random.fold_in(key, 23)
    return root_matrices(key, 0.6, 1.6).astype(jnp.bfloat16)


def level_of(stream_key, dims, cuts, low, top_value):
    gain = 1.0
    for dim, parts in cuts:
        heights = jax.random.uniform(jax.random.fold_in(jax.random.fold_in(stream_key, 6), dim), (parts,), jnp.float32, low / len(cuts), top_value / len(cuts))
        gain = gain * jnp.repeat(jnp.exp(heights), dims[dim] // parts).reshape((-1,) + (1,) * (len(dims) - 1 - dim))
    return gain


def scatter_about(key, shape, scale, bound, cuts=(), held_as=jnp.bfloat16):
    result = jax.random.normal(key, shape, jnp.float32) * scale
    if len(cuts) > 0:
        result = level_of(key, shape, cuts, -0.22, 0.18) * result
    return jnp.clip(result, min=-bound, max=bound).astype(held_as)


def setup_inputs(seed: int = 0) -> dict:
    key_list = jax.random.split(jax.random.key(seed), 10)
    saved_inputs = scatter_about(key_list[0], (SECTIONS, MB, TOKENS, D), 1.0, 6.0, ((0, 16), (2, 32)))
    loss_grad = scatter_about(key_list[1], (MB, TOKENS, D), 1.0, 6.0, ((1, 32),))
    w_in = scatter_about(key_list[2], (SECTIONS, D, BLK), D ** -0.5, 0.09375, ((0, 16),))
    w_out = scatter_about(key_list[3], (SECTIONS, BLK, D), BLK ** -0.5, 0.5, ((0, 16),))
    left_root = draw_left_root(jax.random.fold_in(key_list[9], 71), 0)
    right_root = draw_right_root(jax.random.fold_in(key_list[9], 71), 0)
    momentum = scatter_about(key_list[6], (SECTIONS, OWNERS, CAP, BLK, BLK), 1.0, 6.0, ((0, 16), (1, 32)), jnp.float32)
    owned_blocks = draw_owned_blocks(jax.random.fold_in(key_list[9], 71), 0)
    owned_count = draw_owned_count(jax.random.fold_in(key_list[9], 71), 0)
    return {"saved_inputs": saved_inputs, "loss_grad": loss_grad, "w_in": w_in, "w_out": w_out, "left_root": left_root, "right_root": right_root, "momentum": momentum, "owned_blocks": owned_blocks, "owned_count": owned_count}


MOMENTUM_DECAY = 0.9

def silu_slope(values):
    sigma = jax.nn.sigmoid(values)
    return sigma * (1.0 + values * (1.0 - sigma))

def reference(saved_inputs, loss_grad, w_in, w_out, left_root, right_root, momentum, owned_blocks, owned_count):
    upper = loss_grad
    row_blocks = D // BLK
    grads_all = [None] * SECTIONS
    for section in range(SECTIONS - 1, -1, -1):
        inputs = saved_inputs[section].reshape(MB * TOKENS, D)
        flat_upper = upper.reshape(MB * TOKENS, D)
        pre = jnp.dot(inputs, w_in[section], preferred_element_type=jnp.float32)
        act = jax.nn.silu(pre).astype(jnp.bfloat16)
        back = jnp.dot(flat_upper, w_out[section].T, preferred_element_type=jnp.float32)
        pre_grad = (back * silu_slope(pre)).astype(jnp.bfloat16)
        passed = (flat_upper.astype(jnp.float32) + jnp.dot(pre_grad, w_in[section].T, preferred_element_type=jnp.float32)).astype(jnp.bfloat16)
        x_rep = inputs.reshape(MB, OWNERS, TOK, D).astype(jnp.float32)
        g_rep = pre_grad.reshape(MB, OWNERS, TOK, BLK).astype(jnp.float32)
        a_rep = act.reshape(MB, OWNERS, TOK, BLK).astype(jnp.float32)
        u_rep = flat_upper.reshape(MB, OWNERS, TOK, D).astype(jnp.float32)
        part_in = jnp.einsum('mrtd,mrtk->rdk', x_rep, g_rep).astype(jnp.bfloat16)
        part_out = jnp.einsum('mrtk,mrtd->rkd', a_rep, u_rep).astype(jnp.bfloat16)
        part_in, part_out = lax.optimization_barrier((part_in, part_out))
        grad_in = (lax.optimization_barrier(jnp.sum(part_in.astype(jnp.float32), axis=0)) / OWNERS).astype(jnp.bfloat16)
        grad_out = (lax.optimization_barrier(jnp.sum(part_out.astype(jnp.float32), axis=0)) / OWNERS).astype(jnp.bfloat16)
        grad_in, grad_out = lax.optimization_barrier((grad_in, grad_out))
        blocks_in = grad_in.reshape(row_blocks, BLK, BLK)
        blocks_out = grad_out.reshape(BLK, row_blocks, BLK).transpose(1, 0, 2)
        grads_all[section] = jnp.concatenate([blocks_in, blocks_out], axis=0)
        upper = passed.reshape(MB, TOKENS, D)
    new_moms = []
    search_ins = []
    search_outs = []
    slot_index = jnp.arange(CAP, dtype=jnp.int32)
    for section in range(SECTIONS):
        lists = owned_blocks[section]
        live = slot_index[None, :] < owned_count[section][:, None]
        grad_low = jnp.take(grads_all[section], lists.reshape(-1), axis=0).reshape(OWNERS, CAP, BLK, BLK)
        grad_low = jnp.where(live[:, :, None, None], grad_low, jnp.zeros((), jnp.bfloat16))
        grad = grad_low.astype(jnp.float32)
        first = jnp.einsum('okij,okjl->okil', left_root[section], grad_low, preferred_element_type=jnp.float32)
        right = right_root[section].astype(jnp.float32)
        precond = jnp.einsum('okij,okjl->okil', first, right, precision=lax.Precision.HIGHEST)
        grad_sq = lax.optimization_barrier(jnp.sum(grad * grad, axis=(2, 3)))
        pre_sq = lax.optimization_barrier(jnp.sum(precond * precond, axis=(2, 3)))
        direction = precond * (jnp.sqrt(grad_sq) * lax.rsqrt(pre_sq + 1e-06))[:, :, None, None]
        moved = MOMENTUM_DECAY * momentum[section] + direction
        new_mom = jnp.where(live[:, :, None, None], moved, momentum[section])
        new_moms.append(new_mom)
        search = new_mom.astype(jnp.bfloat16).reshape(OWNERS * CAP, BLK, BLK)
        matches = (lists.reshape(-1)[:, None] == jnp.arange(NBLK, dtype=jnp.int32)[None, :]) & live.reshape(-1)[:, None]
        position = lax.optimization_barrier(jnp.sum(jnp.where(matches, jnp.arange(OWNERS * CAP, dtype=jnp.int32)[:, None], 0), axis=0)).astype(jnp.int32)
        placed = jnp.take(search, position, axis=0)
        search_ins.append(placed[:row_blocks].reshape(D, BLK))
        search_outs.append(placed[row_blocks:].transpose(1, 0, 2).reshape(BLK, D))
    return (jnp.stack(new_moms), jnp.stack(search_ins), jnp.stack(search_outs))
```

```python
import functools

import jax
import jax.numpy as jnp
from jax import lax
from jax.experimental import pallas as pl
from jax.experimental.pallas import tpu as pltpu
from jax.sharding import PartitionSpec as P

MOMENTUM_DECAY = 0.9
MESH = pl.DeviceIdType.MESH
BF16 = jnp.bfloat16
F32 = jnp.float32
COPIES = 160


def dot_nn(a, b):
    return lax.dot_general(a, b, (((1,), (0,)), ((), ())), preferred_element_type=F32)


def dot_nt(a, b):
    return lax.dot_general(a, b, (((1,), (1,)), ((), ())), preferred_element_type=F32)


def silu_slope(values):
    sigma = jax.nn.sigmoid(values)
    return sigma * (1.0 + values * (1.0 - sigma))


def kernel(
    sections,
    x_ref, gl_ref, win_ref, wout_ref, left_ref, right_ref, mom_ref, lists, count,
    newmom_ref, search_in_ref, search_out_ref,
    wz, pg, slope, acc, act_t,
    m_p, m_rc, m_q, m_ra, m_t, m_rb, m_o,
    c_p, c_rc, c_q, c_ra, c_t, c_rb, c_o,
    i_p, i_rc, i_q, i_ra, i_t, i_rb,
    o_p, o_rc, o_q, o_ra, o_t, o_rb,
    r_x, r_pk, r_rk, r_sum, r_rc, r_home,
    d_x, d_pk, d_rk,
    send, recv, z_send, z_recv, p_send, p_recv,
):
    s = lax.axis_index("section")
    dp = lax.axis_index("dp")
    c = lax.rem(dp, 2)
    y = lax.rem(dp // 2, 4)
    x = dp // 8
    last = sections - 1
    first_of = (x, y)
    second_of = (y, x)
    wide = s <= last - 9
    ids = {}

    def sid(key):
        return ids.setdefault(key, len(ids))

    def device(h, a, b):
        return (a * 4 + b) * 2 + c if h == 0 else (b * 4 + a) * 2 + c

    def remote(key, source, target, peer):
        number = sid(key)
        return pltpu.make_async_remote_copy(
            src_ref=source, dst_ref=target, send_sem=send.at[number], recv_sem=recv.at[number],
            device_id={"dp": peer}, device_id_type=MESH,
        )

    sibling = dp + 1 - 2 * c

    def peer_first(h, i):
        a = lax.rem(first_of[h] + i, 4)
        return a, device(h, a, second_of[h])

    def peer_second(h, i):
        b = lax.rem(second_of[h] + i, 4)
        return b, device(h, first_of[h], b)

    def go(copies):
        for copy in copies:
            copy.start()

    def land(copies):
        for copy in copies:
            copy.wait_recv()

    def sent(copies):
        for copy in copies:
            copy.wait_send()

    barrier = pltpu.get_barrier_semaphore()
    greeted = [sibling]
    for h in range(2):
        for i in range(1, 4):
            greeted.append(peer_first(h, i)[1])
    for peer in greeted:
        pl.semaphore_signal(barrier, inc=1, device_id={"dp": peer}, device_id_type=MESH)
    below = lax.rem(s + last, sections)
    above = lax.rem(s + 1, sections)
    for peer in (below, above):
        pl.semaphore_signal(barrier, inc=1, device_id={"section": peer}, device_id_type=MESH)
    pl.semaphore_wait(barrier, 9)

    def slice_copy(index):
        return pltpu.make_async_remote_copy(
            src_ref=wz.at[index], dst_ref=wz.at[index],
            send_sem=z_send.at[index], recv_sem=z_recv.at[index],
            device_id={"section": below}, device_id_type=MESH,
        )

    def pass_copy(index):
        return pltpu.make_async_remote_copy(
            src_ref=pg.at[index], dst_ref=pg.at[index],
            send_sem=p_send.at[index], recv_sem=p_recv.at[index],
            device_id={"section": below}, device_id_type=MESH,
        )

    my_columns = pl.ds(pl.multiple_of(dp * 128, 128), 128)
    wz[s] = win_ref[my_columns, :]

    @pl.when(s > 0)
    def _():
        slice_copy(s).start()

    for h in range(2):
        for k in range(4):
            rows = pl.ds(h * 64, 64)
            at = first_of[h] * 4 + k
            r_x[h, at, 0] = left_ref[k, rows]
            r_x[h, at, 1] = right_ref[k, rows]
            r_x[h, at, 2] = mom_ref[k, rows].astype(BF16)

    def roots_first():
        copies = []
        for h in range(2):
            mine = r_x.at[h, pl.ds(first_of[h] * 4, 4)]
            for i in range(1, 4):
                copies.append(remote(("ra", h, i), mine, mine, peer_first(h, i)[1]))
        return copies

    def roots_second():
        copies = []
        for h in range(2):
            for i in range(1, 4):
                b, peer = peer_second(h, i)
                copies.append(remote(("rb", h, i), r_pk.at[h, b], r_rk.at[h, i - 1], peer))
        return copies

    def roots_pair():
        return [remote(("rc",), r_sum.at[:, 1 - c], r_rc, sibling)]

    def roots_pack():
        land(roots_first())
        for h in range(2):
            def target(t, carry):
                b, core, kind = t // 4, lax.rem(t // 2, 2), lax.rem(t, 2)
                if h == 0:
                    place = (first_of[h] * 4 + b) * 2 + core
                else:
                    place = (b * 4 + first_of[h]) * 2 + core
                block = kind * 32 + place
                index = jnp.int32(0)
                found = jnp.int32(0)
                for a in range(4):
                    owner = device(h, a, second_of[h])
                    held = count[owner]
                    for k in range(4):
                        hit = (lists[owner * 4 + k] == block) & (held > k)
                        index = index + jnp.where(hit, a * 4 + k, 0)
                        found = found + jnp.where(hit, 1, 0)
                value = r_x[h, index]
                r_pk[h, b, core, kind] = jnp.where(found > 0, value, jnp.zeros_like(value))
                return carry
            lax.fori_loop(0, 16, target, 0)
        go(roots_second())

    pl.when(s <= 7)(lambda: go(roots_first()))

    pre = dot_nn(x_ref[...], win_ref[...])
    slope[...] = silu_slope(pre)
    act = jax.nn.silu(pre)
    act_t[...] = act.T.astype(BF16)
    acc[...] = dot_nt(gl_ref[...], wout_ref[...])

    @pl.when(s == last)
    def _():
        pg[s] = (acc[...] * slope[...]).astype(BF16)
        pass_copy(s).start()

    m_p[...] = jnp.zeros_like(m_p)
    c_p[...] = jnp.zeros_like(c_p)

    def relay(k, carry):
        index = s + 1 + k
        copy = slice_copy(index)
        copy.wait_recv()
        pl.when(s > 0)(lambda: copy.start())
        product = dot_nn(wout_ref[:, my_columns], wz[index])
        m_p[k] = product.T.astype(BF16).reshape(4, 2, 16, 128)
        return carry

    lax.fori_loop(0, last - s, relay, 0)

    class Sum:
        def __init__(self, name, p, rc, q, ra, t, rb, o):
            self.name, self.p, self.rc, self.q, self.ra = name, p, rc, q, ra
            self.t, self.rb, self.o = t, rb, o

        def at(self, chunk, h):
            return chunk * 8 + h * 4 + first_of[h]

        def copies(self, stage, chunk):
            n = self.name
            if stage == 0:
                return [remote((n, 0, chunk), self.p.at[pl.ds(chunk * 8, 8), :, 1 - c], self.rc.at[pl.ds(chunk * 8, 8)], sibling)]
            if stage == 5:
                mine = self.o.at[pl.ds(chunk * 8, 8), :, c]
                return [remote((n, 5, chunk), mine, mine, sibling)]
            out = []
            for h in range(2):
                for i in range(1, 4):
                    key = (n, stage, chunk, h, i)
                    if stage in (1, 4):
                        a, peer = peer_first(h, i)
                    else:
                        b, peer = peer_second(h, i)
                    if stage == 1:
                        out.append(remote(key, self.q.at[chunk * 8 + h * 4 + a], self.ra.at[chunk, h, i - 1], peer))
                    elif stage == 2:
                        out.append(remote(key, self.t.at[chunk, h, b], self.rb.at[chunk, h, i - 1], peer))
                    elif stage == 3:
                        mine = self.o.at[self.at(chunk, h), second_of[h], c]
                        out.append(remote(key, mine, mine, peer))
                    else:
                        mine = self.o.at[self.at(chunk, h), :, c]
                        out.append(remote(key, mine, mine, peer))
            return out

        def after(self, stage, chunk):
            land(self.copies(stage, chunk))
            if stage == 0:
                part = pl.ds(chunk * 8, 8)
                self.q[part] = (self.p[part, :, c].astype(F32) + self.rc[part].astype(F32)).astype(BF16)
            elif stage == 1:
                for h in range(2):
                    total = self.q[self.at(chunk, h)].astype(F32)
                    for i in range(3):
                        total = total + self.ra[chunk, h, i].astype(F32)
                    self.t[chunk, h] = total.astype(BF16)
            elif stage == 2:
                for h in range(2):
                    total = self.t[chunk, h, second_of[h]].astype(F32)
                    for i in range(3):
                        total = total + self.rb[chunk, h, i].astype(F32)
                    self.o[self.at(chunk, h), second_of[h], c] = total.astype(BF16)
            elif stage == 5:
                mine = self.o

        def start(self, stage):
            go(self.copies(stage, 0))
            pl.when(wide)(lambda: go(self.copies(stage, 1)))

        def finish(self, stage):
            self.after(stage, 0)
            pl.when(wide)(lambda: self.after(stage, 1))

        def drain(self):
            for stage in range(6):
                sent(self.copies(stage, 0))
                pl.when(wide)(lambda: sent(self.copies(stage, 1)))

    class Scatter:
        def __init__(self, name, p, rc, q, ra, t, rb):
            self.name, self.p, self.rc, self.q = name, p, rc, q
            self.ra, self.t, self.rb = ra, t, rb

        def fill(self, left, right_ref):
            def chip(n, carry):
                cx, cy = n // 4, lax.rem(n, 4)
                columns = pl.ds(pl.multiple_of(n * 256, 256), 256)
                product = dot_nn(left, right_ref[:, columns]).astype(BF16)
                for core in range(2):
                    block = product[:, core * 128:(core + 1) * 128]
                    self.p[0, cx, cy, core] = block[:64]
                    self.p[1, cy, cx, core] = block[64:]
                return carry
            lax.fori_loop(0, 16, chip, 0)

        def copies(self, stage):
            n = self.name
            if stage == 0:
                return [remote((n, 0), self.p.at[:, :, :, 1 - c], self.rc, sibling)]
            out = []
            for h in range(2):
                for i in range(1, 4):
                    if stage == 1:
                        a, peer = peer_first(h, i)
                        out.append(remote((n, 1, h, i), self.q.at[h, a], self.ra.at[h, i - 1], peer))
                    else:
                        b, peer = peer_second(h, i)
                        out.append(remote((n, 2, h, i), self.t.at[h, b], self.rb.at[h, i - 1], peer))
            return out

        def start(self, stage):
            go(self.copies(stage))

        def finish(self, stage):
            land(self.copies(stage))
            if stage == 0:
                for h in range(2):
                    for a in range(4):
                        self.q[h, a] = (self.p[h, a, :, c].astype(F32) + self.rc[h, a].astype(F32)).astype(BF16)
            elif stage == 1:
                for h in range(2):
                    total = self.q[h, first_of[h]].astype(F32)
                    for i in range(3):
                        total = total + self.ra[h, i].astype(F32)
                    self.t[h] = total.astype(BF16)

        def result(self):
            halves = []
            for h in range(2):
                total = self.t[h, second_of[h]].astype(F32)
                for i in range(3):
                    total = total + self.rb[h, i].astype(F32)
                halves.append(total)
            return jnp.concatenate(halves, axis=0)

        def drain(self):
            for stage in range(3):
                sent(self.copies(stage))

    m_sum = Sum("m", m_p, m_rc, m_q, m_ra, m_t, m_rb, m_o)
    c_sum = Sum("c", c_p, c_rc, c_q, c_ra, c_t, c_rb, c_o)
    into = Scatter("i", i_p, i_rc, i_q, i_ra, i_t, i_rb)
    outof = Scatter("o", o_p, o_rc, o_q, o_ra, o_t, o_rb)

    @pl.when(s < last)
    def _():
        m_sum.start(0)
        m_sum.finish(0)
        m_sum.start(1)

    outof.fill(act_t[...], gl_ref)
    outof.start(0)

    @pl.when(s < last)
    def _():
        m_sum.finish(1)
        for stage in range(2, 6):
            m_sum.start(stage)
            m_sum.finish(stage)

    outof.finish(0)
    outof.start(1)

    @pl.when(s > 7)
    def _():
        go(roots_first())

    @pl.when(s <= 7)
    def _():
        roots_pack()

    def add_one(index):
        k = index - s - 1
        acc[...] += dot_nn(pg[index], m_o[k].reshape(128, 128))

    def cross(index):
        k = index - s - 1
        c_p[k] = dot_nn(act_t[...], pg[index]).astype(BF16).reshape(4, 2, 16, 128)

    def arrive(index):
        copy = pass_copy(index)
        copy.wait_recv()
        pl.when(s > 0)(lambda: copy.start())
        add_one(index)

    def link(n, carry):
        arrive(last - n)
        cross(last - n)
        return carry

    lax.fori_loop(0, last - s - 1, link, 0)

    @pl.when(s < last)
    def _():
        arrive(s + 1)
        pg[s] = (acc[...] * slope[...]).astype(BF16)
        pl.when(s > 0)(lambda: pass_copy(s).start())
        cross(s + 1)
        c_sum.start(0)

    into.fill(pg[s].astype(F32).T.astype(BF16), x_ref)
    into.start(0)
    outof.finish(1)
    outof.start(2)

    @pl.when(s < last)
    def _():
        c_sum.finish(0)
        c_sum.start(1)

    into.finish(0)
    into.start(1)

    @pl.when(s < last)
    def _():
        c_sum.finish(1)
        c_sum.start(2)
        c_sum.finish(2)
        c_sum.start(3)

    into.finish(1)
    into.start(2)

    @pl.when(s < last)
    def _():
        c_sum.finish(3)
        c_sum.start(4)

    @pl.when(s > 7)
    def _():
        roots_pack()

    land(roots_second())
    for h in range(2):
        total = r_pk[h, second_of[h]].astype(F32)
        for i in range(3):
            total = total + r_rk[h, i].astype(F32)
        r_sum[h] = total.astype(BF16)
    go(roots_pair())

    into.finish(2)
    land(roots_pair())
    for h in range(2):
        merged = (r_sum[h, c].astype(F32) + r_rc[h].astype(F32)).astype(BF16)
        for kind in range(2):
            for what in range(3):
                r_home[kind, what, pl.ds(h * 64, 64)] = merged[kind, what]

    def direct(kind, grad32, out_ref):
        grad = grad32.astype(BF16)
        exact = grad.astype(F32)
        first = dot_nn(r_home[kind, 0], grad)
        high = first.astype(BF16)
        low = (first - high.astype(F32)).astype(BF16)
        right = r_home[kind, 1]
        precond = dot_nn(high, right) + dot_nn(low, right)
        grad_sq = jnp.sum(jnp.sum(exact * exact, axis=1, keepdims=True), axis=0, keepdims=True)
        pre_sq = jnp.sum(jnp.sum(precond * precond, axis=1, keepdims=True), axis=0, keepdims=True)
        direction = precond * (jnp.sqrt(grad_sq) * lax.rsqrt(pre_sq + 1e-06))
        out_ref[...] = (MOMENTUM_DECAY * r_home[kind, 2].astype(F32) + direction).astype(BF16)
        rounded = direction.astype(BF16)
        for h in range(2):
            d_x[h, first_of[h], c, kind] = rounded[h * 64:(h + 1) * 64]

    direct(0, into.result().T * (1.0 / 32), search_in_ref)

    outof.finish(2)
    acc[...] = outof.result()

    @pl.when(s < last)
    def _():
        c_sum.finish(4)
        c_sum.start(5)
        c_sum.finish(5)

        def term(k, carry):
            acc[...] += dot_nt(c_o[k].reshape(128, 128), wz[s + 1 + k])
            return carry
        lax.fori_loop(0, last - s, term, 0)

    direct(1, acc[...] * (1.0 / 32), search_out_ref)

    def way_first():
        copies = []
        for h in range(2):
            mine = d_x.at[h, first_of[h], c]
            for i in range(1, 4):
                copies.append(remote(("da", h, i), mine, mine, peer_first(h, i)[1]))
        return copies

    def way_pair():
        mine = d_x.at[:, :, c]
        return [remote(("dc",), mine, mine, sibling)]

    def way_second():
        copies = []
        for h in range(2):
            for i in range(1, 4):
                b, peer = peer_second(h, i)
                copies.append(remote(("db", h, i), d_pk.at[h, b], d_rk.at[h, i - 1], peer))
        return copies

    go(way_first())
    land(way_first())
    go(way_pair())
    land(way_pair())
    for h in range(2):
        def slot(t, carry):
            b, k = t // 4, lax.rem(t, 4)
            owner = device(h, first_of[h], b)
            block = lists[owner * 4 + k]
            kind = block // 32
            hx, hy, core = lax.rem(block // 8, 4), lax.rem(block // 2, 4), lax.rem(block, 2)
            a, row = (hx, hy) if h == 0 else (hy, hx)
            here = (row == second_of[h]) & (count[owner] > k)
            value = d_x[h, a, core, kind]
            d_pk[h, b, k] = jnp.where(here, value, jnp.zeros_like(value))
            return carry
        lax.fori_loop(0, 16, slot, 0)
    go(way_second())
    land(way_second())
    for h in range(2):
        total = d_pk[h, second_of[h]].astype(F32)
        for i in range(3):
            total = total + d_rk[h, i].astype(F32)
        rows = pl.ds(h * 64, 64)
        for k in range(4):
            old = mom_ref[k, rows]
            new = MOMENTUM_DECAY * old + total[k]
            newmom_ref[k, rows] = jnp.where(count[dp] > k, new, old)

    @pl.when(s > 0)
    def _():
        def leave(n, carry):
            slice_copy(s + n).wait_send()
            pass_copy(s + n).wait_send()
            return carry
        lax.fori_loop(0, sections - s, leave, 0)

    @pl.when(s < last)
    def _():
        m_sum.drain()
        c_sum.drain()
    into.drain()
    outof.drain()
    sent(roots_first())
    sent(roots_second())
    sent(roots_pair())
    sent(way_first())
    sent(way_pair())
    sent(way_second())


def on_device(
    sections, saved_inputs, loss_grad, w_in, w_out, left_root, right_root, momentum, owned_blocks, owned_count
):
    vmem = pl.BlockSpec(memory_space=pltpu.VMEM)
    smem = pl.BlockSpec(memory_space=pltpu.SMEM)

    def room(*shape, kind=BF16):
        return pltpu.VMEM(shape, kind)

    def sum_room():
        return [
            room(16, 4, 2, 16, 128), room(16, 4, 16, 128), room(16, 4, 16, 128),
            room(2, 2, 3, 4, 16, 128), room(2, 2, 4, 16, 128), room(2, 2, 3, 16, 128),
            room(16, 4, 2, 16, 128),
        ]

    def scatter_room():
        return [
            room(2, 4, 4, 2, 64, 128), room(2, 4, 4, 64, 128), room(2, 4, 4, 64, 128),
            room(2, 3, 4, 64, 128), room(2, 4, 64, 128), room(2, 3, 64, 128),
        ]

    scratch = (
        [room(sections, 128, 128), room(sections, 128, 128), room(128, 128, kind=F32), room(128, 128, kind=F32), room(128, 128)]
        + sum_room() + sum_room() + scatter_room() + scatter_room()
        + [
            room(2, 16, 3, 64, 128), room(2, 4, 2, 2, 3, 64, 128), room(2, 3, 2, 2, 3, 64, 128),
            room(2, 2, 2, 3, 64, 128), room(2, 2, 3, 64, 128), room(2, 3, 128, 128),
            room(2, 4, 2, 2, 64, 128), room(2, 4, 4, 64, 128), room(2, 3, 4, 64, 128),
        ]
        + [pltpu.SemaphoreType.DMA((COPIES,))] * 2
        + [pltpu.SemaphoreType.DMA((sections,))] * 4
    )
    new_mom, search_in, search_out = pl.pallas_call(
        functools.partial(kernel, sections),
        out_shape=(
            jax.ShapeDtypeStruct((4, 128, 128), F32),
            jax.ShapeDtypeStruct((128, 128), BF16),
            jax.ShapeDtypeStruct((128, 128), BF16),
        ),
        in_specs=[vmem] * 7 + [smem] * 2,
        out_specs=(vmem, vmem, vmem),
        scratch_shapes=scratch,
        compiler_params=pltpu.CompilerParams(
            collective_id=0, has_side_effects=True, vmem_limit_bytes=48 * 1024 * 1024
        ),
        name="drain",
    )(
        saved_inputs.reshape(128, 4096), loss_grad.reshape(128, 4096), w_in[0], w_out[0],
        left_root[0, 0], right_root[0, 0], momentum[0, 0],
        owned_blocks.reshape(128), owned_count.reshape(32),
    )
    return new_mom[None, None], search_in[None], search_out[None]


def solution(mesh):
    placed = (
        P("section", None, "dp", None),
        P(None, "dp", None),
        P("section", None, None),
        P("section", None, None),
        P("section", "dp", None, None, None),
        P("section", "dp", None, None, None),
        P("section", "dp", None, None, None),
        P("section", None, None),
        P("section", None),
    )
    return jax.shard_map(
        functools.partial(on_device, mesh.shape["section"]),
        mesh=mesh,
        in_specs=placed,
        out_specs=(
            P("section", "dp", None, None, None),
            P("section", "dp", None),
            P("section", None, "dp"),
        ),
        check_vma=False,
    )
```

```python
import functools

import jax
import jax.numpy as jnp
from jax import lax
from jax.experimental import pallas as pl
from jax.experimental.pallas import tpu as pltpu
from jax.sharding import PartitionSpec as P

MOMENTUM_DECAY = 0.9
MESH = pl.DeviceIdType.MESH
BF16 = jnp.bfloat16
F32 = jnp.float32
COPIES = 72
EARLY = 3
SOON = 8


def dot_nn(a, b):
    return lax.dot_general(a, b, (((1,), (0,)), ((), ())), preferred_element_type=F32)


def dot_nt(a, b):
    return lax.dot_general(a, b, (((1,), (1,)), ((), ())), preferred_element_type=F32)


def silu_slope(values):
    sigma = jax.nn.sigmoid(values)
    return sigma * (1.0 + values * (1.0 - sigma))


def kernel(
    sections,
    x_hbm, gl_hbm, win_hbm, wout_hbm, left_hbm, right_hbm, mom_hbm, lists_ref, count_ref,
    newmom_ref, search_in_ref, search_out_ref,
    x_ref, gl_ref, win_ref, wout_ref, mom_ref,
    wz, pg, slope, base, acc, acc_out, act_t, slope_next, acc_next, m_next,
    m_p, m_rc, m_o,
    c_p, c_rc, c_o,
    i_p, i_rc, i_q, i_ra, i_t, i_rb,
    o_p, o_rc, o_q, o_ra, o_t, o_rb,
    r_x, r_pk, r_rk, r_sum, r_rc, r_home,
    d_x, d_pk, d_rk,
    local, send, recv, z_near, z_far, z_recv, p_near, p_far, p_recv, n_send, n_recv, b_send, b_recv,
):
    s = lax.axis_index("section")
    dp = lax.axis_index("dp")
    c = lax.rem(dp, 2)
    y = lax.rem(dp // 2, 4)
    x = dp // 8
    last = sections - 1
    first_of = (x, y)
    second_of = (y, x)
    wide = s <= last - 9
    ids = {}

    def sid(key):
        return ids.setdefault(key, len(ids))

    def device(h, a, b):
        return (a * 4 + b) * 2 + c if h == 0 else (b * 4 + a) * 2 + c

    def remote(key, source, target, peer):
        number = sid(key)
        return pltpu.make_async_remote_copy(
            src_ref=source, dst_ref=target, send_sem=send.at[number], recv_sem=recv.at[number],
            device_id={"dp": peer}, device_id_type=MESH,
        )

    sibling = dp + 1 - 2 * c

    def peer_first(h, i):
        a = lax.rem(first_of[h] + i, 4)
        return a, device(h, a, second_of[h])

    def peer_second(h, i):
        b = lax.rem(second_of[h] + i, 4)
        return b, device(h, first_of[h], b)

    def go(copies):
        for copy in copies:
            copy.start()

    def land(copies):
        for copy in copies:
            copy.wait_recv()

    def sent(copies):
        for copy in copies:
            copy.wait_send()

    barrier = pltpu.get_barrier_semaphore()

    def greet(i, carry):
        pl.semaphore_signal(barrier, inc=1, device_id={"dp": lax.rem(dp + i, 32)}, device_id_type=MESH)
        return carry

    lax.fori_loop(1, 32, greet, 0)
    below = lax.rem(s + last, sections)
    below_two = lax.rem(s + last - 1, sections)
    even = lax.rem(s, 2) == 0
    for peer in (below, below_two, lax.rem(s + 1, sections), lax.rem(s + 2, sections)):
        pl.semaphore_signal(barrier, inc=1, device_id={"section": peer}, device_id_type=MESH)

    fetches = {}

    def fetch(name, source, target):
        fetches[name] = pltpu.make_async_copy(source, target, local.at[len(fetches)])
        fetches[name].start()

    fetch("x", x_hbm, x_ref)
    fetch("win", win_hbm, win_ref)
    fetch("gl", gl_hbm, gl_ref)
    fetch("wout", wout_hbm, wout_ref)
    fetch("mom", mom_hbm, mom_ref)
    for h in range(2):
        rows = pl.ds(h * 64, 64)
        slots = pl.ds(first_of[h] * 4, 4)
        fetch(("left", h), left_hbm.at[:, rows], r_x.at[h, slots, 0])
        fetch(("right", h), right_hbm.at[:, rows], r_x.at[h, slots, 1])

    pl.semaphore_wait(barrier, 35)

    def to_section(source, target, send_sem, recv_sem, peer):
        return pltpu.make_async_remote_copy(
            src_ref=source, dst_ref=target, send_sem=send_sem, recv_sem=recv_sem,
            device_id={"section": peer}, device_id_type=MESH,
        )

    def slice_near(index):
        return to_section(wz.at[index], wz.at[index], z_near.at[index], z_recv.at[index], below)

    def slice_far(index):
        return to_section(wz.at[index], wz.at[index], z_far.at[index], z_recv.at[index], below_two)

    my_columns = pl.ds(pl.multiple_of(dp * 128, 128), 128)

    def own_near():
        return to_section(win_hbm.at[my_columns], wz.at[s], z_near.at[s], z_recv.at[s], below)

    def own_far():
        return to_section(win_hbm.at[my_columns], wz.at[s], z_far.at[s], z_recv.at[s], below_two)

    def pass_near(index):
        return to_section(pg.at[index], pg.at[index], p_near.at[index], p_recv.at[index], below)

    def pass_far(index):
        return to_section(pg.at[index], pg.at[index], p_far.at[index], p_recv.at[index], below_two)

    def share_state():
        return [
            to_section(base, acc_next, b_send.at[0], b_recv.at[0], below),
            to_section(slope, slope_next, b_send.at[1], b_recv.at[1], below),
        ]

    def places(k):
        if isinstance(k, int):
            return k // 8, k // 4 % 2, k % 4
        return k // 8, lax.rem(k // 4, 2), lax.rem(k, 4)

    def share_product(k):
        return to_section(m_o.at[places(k)], m_next.at[k], n_send.at[k], n_recv.at[k], below)

    pl.when(s > 1)(lambda: own_far().start())
    pl.when(s > 0)(lambda: own_near().start())

    def roots_first():
        copies = []
        for h in range(2):
            mine = r_x.at[h, pl.ds(first_of[h] * 4, 4)]
            for i in range(1, 4):
                copies.append(remote(("ra", h, i), mine, mine, peer_first(h, i)[1]))
        return copies

    def roots_second():
        copies = []
        for h in range(2):
            for i in range(1, 4):
                b, peer = peer_second(h, i)
                copies.append(remote(("rb", h, i), r_pk.at[h, b], r_rk.at[h, i - 1], peer))
        return copies

    def roots_pair():
        return [remote(("rc",), r_sum.at[:, 1 - c], r_rc, sibling)]

    def roots_pack():
        land(roots_first())
        for h in range(2):
            def target(t, carry):
                b, core, kind = t // 4, lax.rem(t // 2, 2), lax.rem(t, 2)
                if h == 0:
                    place = (first_of[h] * 4 + b) * 2 + core
                else:
                    place = (b * 4 + first_of[h]) * 2 + core
                block = kind * 32 + place
                index = jnp.int32(0)
                found = jnp.int32(0)
                for a in range(4):
                    owner = device(h, a, second_of[h])
                    held = count_ref[0, owner]
                    for k in range(4):
                        hit = (lists_ref[0, k, owner] == block) & (held > k)
                        index = index + jnp.where(hit, a * 4 + k, 0)
                        found = found + jnp.where(hit, 1, 0)
                value = r_x[h, index]
                r_pk[h, b, core, kind] = jnp.where(found > 0, value, jnp.zeros_like(value))
                return carry
            lax.fori_loop(0, 16, target, 0)
        go(roots_second())

    fetches["x"].wait()
    fetches["win"].wait()
    pre = dot_nn(x_ref[...], win_ref[...])
    slope[...] = silu_slope(pre)
    act = jax.nn.silu(pre)
    act_t[...] = act.T.astype(BF16)
    fetches["gl"].wait()
    fetches["wout"].wait()
    base[...] = dot_nt(gl_ref[...], wout_ref[...])
    acc[...] = base[...]

    @pl.when(~even)
    def _():
        go(share_state())

    fetches["mom"].wait()
    for h in range(2):
        for k in range(4):
            r_x[h, first_of[h] * 4 + k, 2] = mom_ref[k, pl.ds(h * 64, 64)].astype(BF16)
        fetches[("left", h)].wait()
        fetches[("right", h)].wait()

    @pl.when(s <= SOON)
    def _():
        go(roots_first())

    wz[sections:] = jnp.zeros_like(wz[sections:])
    m_p[...] = jnp.zeros_like(m_p)
    c_p[...] = jnp.zeros_like(c_p)

    class Sum:
        def __init__(self, name, p, rc, o):
            self.name, self.p, self.rc, self.o = name, p, rc, o

        def start(self, stage, first, size):
            number = sid((self.name, stage, first))
            part = pl.ds(first, size)

            def one(i, carry):
                peer = lax.rem(dp + i, 32)
                if stage == 0:
                    source = self.p.at[part, :, peer // 8, lax.rem(peer // 2, 4), lax.rem(peer, 2)]
                    target = self.rc.at[i - 1, part]
                else:
                    source = target = self.o.at[part, :, x, y, c]
                pltpu.make_async_remote_copy(
                    src_ref=source, dst_ref=target, send_sem=send.at[number], recv_sem=recv.at[number],
                    device_id={"dp": peer}, device_id_type=MESH,
                ).start()
                return carry

            lax.fori_loop(1, 32, one, 0)

        def all_bytes(self, sems, stage, first, size):
            number = sid((self.name, stage, first))
            every = self.rc.at[:, pl.ds(first, size)]
            pltpu.make_async_copy(every, every, sems.at[number]).wait()

        def finish(self, stage, first, size):
            self.all_bytes(recv, stage, first, size)
            if stage == 0:
                part = pl.ds(first, size)
                total = self.p[part, :, x, y, c].astype(F32)
                for i in range(31):
                    total = total + self.rc[i, part].astype(F32)
                self.o[part, :, x, y, c] = total.astype(BF16)

        def drain(self, first, size):
            for stage in range(2):
                self.all_bytes(send, stage, first, size)

    class Scatter:
        def __init__(self, name, p, rc, q, ra, t, rb):
            self.name, self.p, self.rc, self.q = name, p, rc, q
            self.ra, self.t, self.rb = ra, t, rb

        def fill(self, left, right_ref):
            def chip(n, carry):
                cx, cy = n // 4, lax.rem(n, 4)
                columns = pl.ds(pl.multiple_of(n * 256, 256), 256)
                product = dot_nn(left, right_ref[:, columns]).astype(BF16)
                for core in range(2):
                    block = product[:, core * 128:(core + 1) * 128]
                    self.p[0, cx, cy, core] = block[:64]
                    self.p[1, cy, cx, core] = block[64:]
                return carry
            lax.fori_loop(0, 16, chip, 0)

        def copies(self, stage):
            n = self.name
            if stage == 0:
                return [remote((n, 0), self.p.at[:, :, :, 1 - c], self.rc, sibling)]
            out = []
            for h in range(2):
                for i in range(1, 4):
                    if stage == 1:
                        a, peer = peer_first(h, i)
                        out.append(remote((n, 1, h, i), self.q.at[h, a], self.ra.at[h, i - 1], peer))
                    else:
                        b, peer = peer_second(h, i)
                        out.append(remote((n, 2, h, i), self.t.at[h, b], self.rb.at[h, i - 1], peer))
            return out

        def start(self, stage):
            go(self.copies(stage))

        def finish(self, stage):
            land(self.copies(stage))
            if stage == 0:
                for h in range(2):
                    for a in range(4):
                        self.q[h, a] = (self.p[h, a, :, c].astype(F32) + self.rc[h, a].astype(F32)).astype(BF16)
            elif stage == 1:
                for h in range(2):
                    total = self.q[h, first_of[h]].astype(F32)
                    for i in range(3):
                        total = total + self.ra[h, i].astype(F32)
                    self.t[h] = total.astype(BF16)

        def result(self):
            halves = []
            for h in range(2):
                total = self.t[h, second_of[h]].astype(F32)
                for i in range(3):
                    total = total + self.rb[h, i].astype(F32)
                halves.append(total)
            return jnp.concatenate(halves, axis=0)

        def drain(self):
            for stage in range(3):
                sent(self.copies(stage))

    m_sum = Sum("m", m_p, m_rc, m_o)
    c_sum = Sum("c", c_p, c_rc, c_o)
    into = Scatter("i", i_p, i_rc, i_q, i_ra, i_t, i_rb)
    outof = Scatter("o", o_p, o_rc, o_q, o_ra, o_t, o_rb)

    def product(t):
        block = dot_nn(wout_ref[:, my_columns], wz[s + t])
        m_p[places(t - 1)] = block.astype(BF16).reshape(4, 2, 16, 128)

    def relay(n, carry):
        odd = 2 * n + 1
        far = 2 * n + 2
        slice_far(s + far).wait_recv()

        @pl.when(s > 1)
        def _():
            slice_far(s + far).start()
            slice_near(s + far).start()

        pl.when(s == 1)(lambda: slice_near(s + far).start())
        slice_near(s + odd).wait_recv()
        product(odd)
        product(far)

        @pl.when(wide & (n == 3))
        def _():
            m_sum.start(0, 0, 1)

        @pl.when(wide & (n == 4))
        def _():
            m_sum.finish(0, 0, 1)
            m_sum.start(1, 0, 1)

        @pl.when(wide & (n == 5))
        def _():
            m_sum.finish(1, 0, 1)
        return carry

    steps = (last - s) // 2
    lax.fori_loop(0, steps, relay, 0)

    @pl.when(even)
    def _():
        slice_near(last).wait_recv()
        product(last - s)

    @pl.when(wide)
    def _():
        @pl.when(steps < 5)
        def _():
            m_sum.finish(0, 0, 1)
            m_sum.start(1, 0, 1)

        m_sum.start(0, 1, 1)
        pl.when(steps < 6)(lambda: m_sum.finish(1, 0, 1))

    pl.when((~wide) & (s < last))(lambda: m_sum.start(0, 0, 1))

    @pl.when(s <= EARLY)
    def _():
        outof.fill(act_t[...], gl_ref)
        outof.start(0)

    @pl.when(wide)
    def _():
        m_sum.finish(0, 1, 1)
        m_sum.start(1, 1, 1)

    @pl.when(s <= EARLY)
    def _():
        outof.finish(0)
        roots_pack()
        outof.start(1)

    pl.when(wide)(lambda: m_sum.finish(1, 1, 1))

    @pl.when((~wide) & (s < last))
    def _():
        m_sum.finish(0, 0, 1)
        m_sum.start(1, 0, 1)
        m_sum.finish(1, 0, 1)

    @pl.when(~even)
    def _():
        def give(k, carry):
            share_product(k).start()
            return carry
        lax.fori_loop(0, last - s, give, 0)

    pl.when(s > SOON)(lambda: go(roots_first()))

    def cross(index):
        c_p[places(index - s - 1)] = dot_nn(act_t[...], pg[index]).astype(BF16).reshape(4, 2, 16, 128)

    def own_term(index):
        return dot_nt(pg[index], m_o[places(index - s - 1)].reshape(128, 128))

    def next_term(index):
        return dot_nt(pg[index], m_next[index - s - 2].reshape(128, 128))

    lowest = (s + 2) // 2

    @pl.when(even)
    def _():
        land(share_state())

        def come(high, low):
            pass_far(high).wait_recv()
            pass_far(low).wait_recv()

            @pl.when(s > 0)
            def _():
                pass_far(high).start()
                pass_far(low).start()

        def products(high, low):
            share_product(high - s - 2).wait_recv()
            share_product(low - s - 2).wait_recv()

        def collect(n, carry):
            high, low = 15 - 2 * n, 14 - 2 * n
            come(high, low)

            @pl.when(s > 0)
            def _():
                pass_near(high).start()
                pass_near(low).start()
            return carry

        def add(n, carry):
            high, low = 15 - 2 * n, 14 - 2 * n
            products(high, low)
            acc_next[...] += next_term(high) + next_term(low)
            acc[...] += own_term(high) + own_term(low)
            return carry

        lax.fori_loop(0, 7 - lowest, collect, 0)
        lax.fori_loop(0, 7 - lowest, add, 0)

        @pl.when(s < last - 1)
        def _():
            high, low = 2 * lowest + 1, 2 * lowest
            products(high, low)
            come(high, low)
            pg[s + 1] = ((acc_next[...] + next_term(high) + next_term(low)) * slope_next[...]).astype(BF16)
            pl.when(s > 0)(lambda: pass_far(s + 1).start())
            pg[s] = ((acc[...] + own_term(high) + own_term(low) + own_term(s + 1)) * slope[...]).astype(BF16)

            @pl.when(s > 0)
            def _():
                pass_far(s).start()
                for index in (high, low, s + 1, s):
                    pass_near(index).start()

        @pl.when(s == last - 1)
        def _():
            pg[s + 1] = (acc_next[...] * slope_next[...]).astype(BF16)
            pass_far(s + 1).start()
            pg[s] = ((acc[...] + own_term(s + 1)) * slope[...]).astype(BF16)
            pass_far(s).start()
            pass_near(s + 1).start()
            pass_near(s).start()

    @pl.when(~even)
    def _():
        def collect(n, carry):
            high, low = 15 - 2 * n, 14 - 2 * n
            pass_far(high).wait_recv()
            pass_far(low).wait_recv()
            acc[...] += own_term(high) + own_term(low)
            return carry

        lax.fori_loop(0, 8 - lowest, collect, 0)
        pg[s] = (acc[...] * slope[...]).astype(BF16)

    def cross_two(n, carry):
        cross(s + 1 + 2 * n)
        cross(s + 2 + 2 * n)
        return carry

    lax.fori_loop(0, (last - s) // 2, cross_two, 0)
    pl.when(even)(lambda: cross(last))
    pl.when(wide)(lambda: c_sum.start(0, 0, 2))
    pl.when((~wide) & (s < last))(lambda: c_sum.start(0, 0, 1))

    into.fill(pg[s].astype(F32).T.astype(BF16), x_ref)
    into.start(0)

    into.finish(0)
    into.start(1)

    @pl.when(wide)
    def _():
        c_sum.finish(0, 0, 2)
        c_sum.start(1, 0, 2)

    @pl.when((~wide) & (s < last))
    def _():
        c_sum.finish(0, 0, 1)
        c_sum.start(1, 0, 1)

    @pl.when(s > EARLY)
    def _():
        roots_pack()
        outof.fill(act_t[...], gl_ref)
        outof.start(0)
        outof.finish(0)
        outof.start(1)

    outof.finish(1)
    outof.start(2)
    into.finish(1)
    into.start(2)

    land(roots_second())
    for h in range(2):
        total = r_pk[h, second_of[h]].astype(F32)
        for i in range(3):
            total = total + r_rk[h, i].astype(F32)
        r_sum[h] = total.astype(BF16)
    go(roots_pair())

    def terms(first):
        total = acc_out[...]
        for k in range(first, first + 8):
            total = total + dot_nt(c_o[places(k)].reshape(128, 128), wz[s + 1 + k])
        acc_out[...] = total

    outof.finish(2)
    acc_out[...] = outof.result()

    into.finish(2)
    land(roots_pair())
    for h in range(2):
        merged = (r_sum[h, c].astype(F32) + r_rc[h].astype(F32)).astype(BF16)
        for kind in range(2):
            for what in range(3):
                r_home[kind, what, pl.ds(h * 64, 64)] = merged[kind, what]

    def direct(kind, grad32, out_ref):
        grad = grad32.astype(BF16)
        exact = grad.astype(F32)
        first = dot_nn(r_home[kind, 0], grad)
        high = first.astype(BF16)
        low = (first - high.astype(F32)).astype(BF16)
        right = r_home[kind, 1]
        precond = dot_nn(high, right) + dot_nn(low, right)
        grad_sq = jnp.sum(jnp.sum(exact * exact, axis=1, keepdims=True), axis=0, keepdims=True)
        pre_sq = jnp.sum(jnp.sum(precond * precond, axis=1, keepdims=True), axis=0, keepdims=True)
        direction = precond * (jnp.sqrt(grad_sq) * lax.rsqrt(pre_sq + 1e-06))
        out_ref[...] = (MOMENTUM_DECAY * r_home[kind, 2].astype(F32) + direction).astype(BF16)
        rounded = direction.astype(BF16)
        for h in range(2):
            d_x[h, first_of[h], c, kind] = rounded[h * 64:(h + 1) * 64]

    direct(0, into.result().T * (1.0 / 32), search_in_ref)

    def way_first(kind):
        copies = []
        for h in range(2):
            mine = d_x.at[h, first_of[h], c, kind]
            for i in range(1, 4):
                copies.append(remote(("da", h, i, kind), mine, mine, peer_first(h, i)[1]))
        return copies

    go(way_first(0))

    @pl.when(wide)
    def _():
        c_sum.finish(1, 0, 2)
        terms(8)
        terms(0)

    @pl.when((~wide) & (s < last))
    def _():
        c_sum.finish(1, 0, 1)
        terms(0)

    direct(1, acc_out[...] * (1.0 / 32), search_out_ref)

    def way_pair():
        mine = d_x.at[:, :, c]
        return [remote(("dc",), mine, mine, sibling)]

    def way_second():
        copies = []
        for h in range(2):
            for i in range(1, 4):
                b, peer = peer_second(h, i)
                copies.append(remote(("db", h, i), d_pk.at[h, b], d_rk.at[h, i - 1], peer))
        return copies

    go(way_first(1))
    land(way_first(0))
    land(way_first(1))
    go(way_pair())
    land(way_pair())
    for h in range(2):
        def slot(t, carry):
            b, k = t // 4, lax.rem(t, 4)
            owner = device(h, first_of[h], b)
            block = lists_ref[0, k, owner]
            kind = block // 32
            hx, hy, core = lax.rem(block // 8, 4), lax.rem(block // 2, 4), lax.rem(block, 2)
            a, row = (hx, hy) if h == 0 else (hy, hx)
            here = (row == second_of[h]) & (count_ref[0, owner] > k)
            value = d_x[h, a, core, kind]
            d_pk[h, b, k] = jnp.where(here, value, jnp.zeros_like(value))
            return carry
        lax.fori_loop(0, 16, slot, 0)
    go(way_second())
    land(way_second())
    for h in range(2):
        total = d_pk[h, second_of[h]].astype(F32)
        for i in range(3):
            total = total + d_rk[h, i].astype(F32)
        rows = pl.ds(h * 64, 64)
        for k in range(4):
            old = mom_ref[k, rows]
            new = MOMENTUM_DECAY * old + total[k]
            newmom_ref[k, rows] = jnp.where(count_ref[0, dp] > k, new, old)

    pl.when(s > 1)(lambda: own_far().wait_send())
    pl.when(s > 0)(lambda: own_near().wait_send())

    def leave(t, carry):
        @pl.when(lax.rem(t, 2) == 0)
        def _():
            pl.when(s > 1)(lambda: slice_far(s + t).wait_send())
            pl.when(s > 0)(lambda: slice_near(s + t).wait_send())
        return carry

    lax.fori_loop(1, sections - s, leave, 0)

    @pl.when(even & (s > 0))
    def _():
        def passed(index, carry):
            pass_far(index).wait_send()
            pass_near(index).wait_send()
            return carry
        lax.fori_loop(s, sections, passed, 0)

    @pl.when(~even)
    def _():
        sent(share_state())

        def given(k, carry):
            share_product(k).wait_send()
            return carry
        lax.fori_loop(0, last - s, given, 0)

    @pl.when(wide)
    def _():
        m_sum.drain(0, 1)
        m_sum.drain(1, 1)
        c_sum.drain(0, 2)

    @pl.when((~wide) & (s < last))
    def _():
        m_sum.drain(0, 1)
        c_sum.drain(0, 1)

    into.drain()
    outof.drain()
    sent(roots_first())
    sent(roots_second())
    sent(roots_pair())
    sent(way_first(0))
    sent(way_first(1))
    sent(way_pair())
    sent(way_second())


def on_device(
    sections, saved_inputs, loss_grad, w_in, w_out, left_root, right_root, momentum, owned_blocks, owned_count
):
    vmem = pl.BlockSpec(memory_space=pltpu.VMEM)
    hbm = pl.BlockSpec(memory_space=pltpu.HBM)
    smem = pl.BlockSpec(memory_space=pltpu.SMEM)

    def room(*shape, kind=BF16):
        return pltpu.VMEM(shape, kind)

    def sum_room():
        return [
            room(2, 2, 4, 4, 2, 16, 128), room(31, 2, 2, 16, 128), room(2, 2, 4, 4, 2, 16, 128),
        ]

    def scatter_room():
        return [
            room(2, 4, 4, 2, 64, 128), room(2, 4, 4, 64, 128), room(2, 4, 4, 64, 128),
            room(2, 3, 4, 64, 128), room(2, 4, 64, 128), room(2, 3, 64, 128),
        ]

    scratch = (
        [
            room(128, 4096), room(128, 4096), room(4096, 128), room(128, 4096), room(4, 128, 128, kind=F32),
            room(sections + 8, 128, 128), room(sections, 128, 128),
            room(128, 128, kind=F32), room(128, 128, kind=F32), room(128, 128, kind=F32), room(128, 128, kind=F32), room(128, 128),
            room(128, 128, kind=F32), room(128, 128, kind=F32), room(16, 4, 2, 16, 128),
        ]
        + sum_room() + sum_room() + scatter_room() + scatter_room()
        + [
            room(2, 16, 3, 64, 128), room(2, 4, 2, 2, 3, 64, 128), room(2, 3, 2, 2, 3, 64, 128),
            room(2, 2, 2, 3, 64, 128), room(2, 2, 3, 64, 128), room(2, 3, 128, 128),
            room(2, 4, 2, 2, 64, 128), room(2, 4, 4, 64, 128), room(2, 3, 4, 64, 128),
        ]
        + [pltpu.SemaphoreType.DMA((9,))]
        + [pltpu.SemaphoreType.DMA((COPIES,))] * 2
        + [pltpu.SemaphoreType.DMA((sections,))] * 8
        + [pltpu.SemaphoreType.DMA((2,))] * 2
    )
    new_mom, search_in, search_out = pl.pallas_call(
        functools.partial(kernel, sections),
        out_shape=(
            jax.ShapeDtypeStruct((4, 128, 128), F32),
            jax.ShapeDtypeStruct((128, 128), BF16),
            jax.ShapeDtypeStruct((128, 128), BF16),
        ),
        in_specs=[hbm] * 7 + [smem] * 2,
        out_specs=(vmem, vmem, vmem),
        scratch_shapes=scratch,
        compiler_params=pltpu.CompilerParams(
            collective_id=0, has_side_effects=True, vmem_limit_bytes=60 * 1024 * 1024
        ),
        name="drain",
    )(
        saved_inputs.reshape(128, 4096), loss_grad.reshape(128, 4096), w_in[0], w_out[0],
        left_root[0, 0], right_root[0, 0], momentum[0, 0],
        jnp.swapaxes(owned_blocks, 1, 2), owned_count,
    )
    return new_mom[None, None], search_in[None], search_out[None]


def solution(mesh):
    placed = (
        P("section", None, "dp", None),
        P(None, "dp", None),
        P("section", None, None),
        P("section", None, None),
        P("section", "dp", None, None, None),
        P("section", "dp", None, None, None),
        P("section", "dp", None, None, None),
        P("section", None, None),
        P("section", None),
    )
    return jax.shard_map(
        functools.partial(on_device, mesh.shape["section"]),
        mesh=mesh,
        in_specs=placed,
        out_specs=(
            P("section", "dp", None, None, None),
            P("section", "dp", None),
            P("section", None, "dp"),
        ),
        check_vma=False,
    )
```

```python
import functools

import jax
import jax.numpy as jnp
from jax import lax
from jax.experimental import pallas as pl
from jax.experimental.pallas import tpu as pltpu
from jax.sharding import PartitionSpec as P

MOMENTUM_DECAY = 0.9
MESH = pl.DeviceIdType.MESH
BF16 = jnp.bfloat16
F32 = jnp.float32
COPIES = 72
EARLY = 3
SOON = 8


def dot_nn(a, b):
    return lax.dot_general(a, b, (((1,), (0,)), ((), ())), preferred_element_type=F32)


def dot_nt(a, b):
    return lax.dot_general(a, b, (((1,), (1,)), ((), ())), preferred_element_type=F32)


def silu_slope(values):
    sigma = jax.nn.sigmoid(values)
    return sigma * (1.0 + values * (1.0 - sigma))


def kernel(
    sections,
    x_hbm, gl_hbm, win_hbm, wout_hbm, left_hbm, right_hbm, mom_hbm, lists_ref, count_ref,
    newmom_ref, search_in_ref, search_out_ref,
    x_ref, gl_ref, win_ref, wout_ref, mom_ref,
    wz, pg, slope, base, acc, acc_out, act_t, slope_next, acc_next, m_next,
    m_p, m_rc, m_o,
    c_p, c_rc, c_o,
    i_p, i_rc, i_q, i_ra, i_t, i_rb,
    o_p, o_rc, o_q, o_ra, o_t, o_rb,
    r_x, r_pk, r_rk, r_sum, r_rc, r_home,
    d_x, d_pk, d_rk,
    local, send, recv, z_near, z_far, z_recv, p_near, p_far, p_recv, n_send, n_recv, b_send, b_recv,
):
    s = lax.axis_index("section")
    dp = lax.axis_index("dp")
    c = lax.rem(dp, 2)
    y = lax.rem(dp // 2, 4)
    x = dp // 8
    last = sections - 1
    first_of = (x, y)
    second_of = (y, x)
    wide = s <= last - 9
    ids = {}

    def sid(key):
        return ids.setdefault(key, len(ids))

    def device(h, a, b):
        return (a * 4 + b) * 2 + c if h == 0 else (b * 4 + a) * 2 + c

    def remote(key, source, target, peer):
        number = sid(key)
        return pltpu.make_async_remote_copy(
            src_ref=source, dst_ref=target, send_sem=send.at[number], recv_sem=recv.at[number],
            device_id={"dp": peer}, device_id_type=MESH,
        )

    sibling = dp + 1 - 2 * c

    def peer_first(h, i):
        a = lax.rem(first_of[h] + i, 4)
        return a, device(h, a, second_of[h])

    def peer_second(h, i):
        b = lax.rem(second_of[h] + i, 4)
        return b, device(h, first_of[h], b)

    def go(copies):
        for copy in copies:
            copy.start()

    def land(copies):
        for copy in copies:
            copy.wait_recv()

    def sent(copies):
        for copy in copies:
            copy.wait_send()

    barrier = pltpu.get_barrier_semaphore()

    def greet(i, carry):
        pl.semaphore_signal(barrier, inc=1, device_id={"dp": lax.rem(dp + i, 32)}, device_id_type=MESH)
        return carry

    lax.fori_loop(1, 32, greet, 0)
    below = lax.rem(s + last, sections)
    below_two = lax.rem(s + last - 1, sections)
    even = lax.rem(s, 2) == 0
    for peer in (below, below_two, lax.rem(s + 1, sections), lax.rem(s + 2, sections)):
        pl.semaphore_signal(barrier, inc=1, device_id={"section": peer}, device_id_type=MESH)

    fetches = {}

    def fetch(name, source, target):
        fetches[name] = pltpu.make_async_copy(source, target, local.at[len(fetches)])
        fetches[name].start()

    fetch("x", x_hbm, x_ref)
    fetch("win", win_hbm, win_ref)
    fetch("gl", gl_hbm, gl_ref)
    fetch("wout", wout_hbm, wout_ref)
    fetch("mom", mom_hbm, mom_ref)
    for h in range(2):
        rows = pl.ds(h * 64, 64)
        slots = pl.ds(first_of[h] * 4, 4)
        fetch(("left", h), left_hbm.at[:, rows], r_x.at[h, slots, 0])
        fetch(("right", h), right_hbm.at[:, rows], r_x.at[h, slots, 1])

    pl.semaphore_wait(barrier, 35)

    def to_section(source, target, send_sem, recv_sem, peer):
        return pltpu.make_async_remote_copy(
            src_ref=source, dst_ref=target, send_sem=send_sem, recv_sem=recv_sem,
            device_id={"section": peer}, device_id_type=MESH,
        )

    def slice_near(index):
        return to_section(wz.at[index], wz.at[index], z_near.at[index], z_recv.at[index], below)

    def slice_far(index):
        return to_section(wz.at[index], wz.at[index], z_far.at[index], z_recv.at[index], below_two)

    my_columns = pl.ds(pl.multiple_of(dp * 128, 128), 128)

    def own_near():
        return to_section(win_hbm.at[my_columns], wz.at[s], z_near.at[s], z_recv.at[s], below)

    def own_far():
        return to_section(win_hbm.at[my_columns], wz.at[s], z_far.at[s], z_recv.at[s], below_two)

    def pass_near(index):
        return to_section(pg.at[index], pg.at[index], p_near.at[index], p_recv.at[index], below)

    def pass_far(index):
        return to_section(pg.at[index], pg.at[index], p_far.at[index], p_recv.at[index], below_two)

    def share_state():
        return [
            to_section(base, acc_next, b_send.at[0], b_recv.at[0], below),
            to_section(slope, slope_next, b_send.at[1], b_recv.at[1], below),
        ]

    def places(k):
        if isinstance(k, int):
            return k // 8, k // 4 % 2, k % 4
        return k // 8, lax.rem(k // 4, 2), lax.rem(k, 4)

    def share_product(k):
        return to_section(m_o.at[places(k)], m_next.at[k], n_send.at[k], n_recv.at[k], below)

    def pair_product(k):
        return pltpu.make_async_remote_copy(
            src_ref=m_next.at[k], dst_ref=m_next.at[k], send_sem=n_send.at[k], recv_sem=n_recv.at[k],
            device_id={"dp": sibling}, device_id_type=MESH,
        )

    pl.when(s > 1)(lambda: own_far().start())
    pl.when(s > 0)(lambda: own_near().start())

    def roots_first():
        copies = []
        for h in range(2):
            mine = r_x.at[h, pl.ds(first_of[h] * 4, 4)]
            for i in range(1, 4):
                copies.append(remote(("ra", h, i), mine, mine, peer_first(h, i)[1]))
        return copies

    def roots_second():
        copies = []
        for h in range(2):
            for i in range(1, 4):
                b, peer = peer_second(h, i)
                copies.append(remote(("rb", h, i), r_pk.at[h, b], r_rk.at[h, i - 1], peer))
        return copies

    def roots_pair():
        return [remote(("rc",), r_sum.at[:, 1 - c], r_rc, sibling)]

    def roots_pack():
        land(roots_first())
        for h in range(2):
            def target(t, carry):
                b, core, kind = t // 4, lax.rem(t // 2, 2), lax.rem(t, 2)
                if h == 0:
                    place = (first_of[h] * 4 + b) * 2 + core
                else:
                    place = (b * 4 + first_of[h]) * 2 + core
                block = kind * 32 + place
                index = jnp.int32(0)
                found = jnp.int32(0)
                for a in range(4):
                    owner = device(h, a, second_of[h])
                    held = count_ref[0, owner]
                    for k in range(4):
                        hit = (lists_ref[0, k, owner] == block) & (held > k)
                        index = index + jnp.where(hit, a * 4 + k, 0)
                        found = found + jnp.where(hit, 1, 0)
                value = r_x[h, index]
                r_pk[h, b, core, kind] = jnp.where(found > 0, value, jnp.zeros_like(value))
                return carry
            lax.fori_loop(0, 16, target, 0)
        go(roots_second())

    fetches["x"].wait()
    fetches["win"].wait()
    pre = dot_nn(x_ref[...], win_ref[...])
    slope[...] = silu_slope(pre)
    act = jax.nn.silu(pre)
    act_t[...] = act.T.astype(BF16)
    fetches["gl"].wait()
    fetches["wout"].wait()
    base[...] = dot_nt(gl_ref[...], wout_ref[...])
    acc[...] = base[...]

    @pl.when(~even)
    def _():
        go(share_state())

    fetches["mom"].wait()
    for h in range(2):
        for k in range(4):
            r_x[h, first_of[h] * 4 + k, 2] = mom_ref[k, pl.ds(h * 64, 64)].astype(BF16)
        fetches[("left", h)].wait()
        fetches[("right", h)].wait()

    @pl.when(s <= SOON)
    def _():
        go(roots_first())

    wz[sections:] = jnp.zeros_like(wz[sections:])
    m_p[...] = jnp.zeros_like(m_p)
    c_p[...] = jnp.zeros_like(c_p)

    class Sum:
        def __init__(self, name, p, rc, o):
            self.name, self.p, self.rc, self.o = name, p, rc, o

        def start(self, stage, first, size):
            number = sid((self.name, stage, first))
            part = pl.ds(first, size)

            def one(i, carry):
                peer = lax.rem(dp + i, 32)
                if stage == 0:
                    source = self.p.at[part, :, peer // 8, lax.rem(peer // 2, 4), lax.rem(peer, 2)]
                    target = self.rc.at[i - 1, part]
                else:
                    source = target = self.o.at[part, :, x, y, c]
                pltpu.make_async_remote_copy(
                    src_ref=source, dst_ref=target, send_sem=send.at[number], recv_sem=recv.at[number],
                    device_id={"dp": peer}, device_id_type=MESH,
                ).start()
                return carry

            lax.fori_loop(1, 32, one, 0)

        def all_bytes(self, sems, stage, first, size):
            number = sid((self.name, stage, first))
            every = self.rc.at[:, pl.ds(first, size)]
            pltpu.make_async_copy(every, every, sems.at[number]).wait()

        def finish(self, stage, first, size):
            self.all_bytes(recv, stage, first, size)
            if stage == 0:
                part = pl.ds(first, size)
                total = self.p[part, :, x, y, c].astype(F32)
                for i in range(31):
                    total = total + self.rc[i, part].astype(F32)
                self.o[part, :, x, y, c] = total.astype(BF16)

        def drain(self, first, size):
            for stage in range(2):
                self.all_bytes(send, stage, first, size)

    class Scatter:
        def __init__(self, name, p, rc, q, ra, t, rb):
            self.name, self.p, self.rc, self.q = name, p, rc, q
            self.ra, self.t, self.rb = ra, t, rb

        def fill(self, left, right_ref):
            def chip(n, carry):
                cx, cy = n // 4, lax.rem(n, 4)
                columns = pl.ds(pl.multiple_of(n * 256, 256), 256)
                product = dot_nn(left, right_ref[:, columns]).astype(BF16)
                for core in range(2):
                    block = product[:, core * 128:(core + 1) * 128]
                    self.p[0, cx, cy, core] = block[:64]
                    self.p[1, cy, cx, core] = block[64:]
                return carry
            lax.fori_loop(0, 16, chip, 0)

        def copies(self, stage):
            n = self.name
            if stage == 0:
                return [remote((n, 0), self.p.at[:, :, :, 1 - c], self.rc, sibling)]
            out = []
            for h in range(2):
                for i in range(1, 4):
                    if stage == 1:
                        a, peer = peer_first(h, i)
                        out.append(remote((n, 1, h, i), self.q.at[h, a], self.ra.at[h, i - 1], peer))
                    else:
                        b, peer = peer_second(h, i)
                        out.append(remote((n, 2, h, i), self.t.at[h, b], self.rb.at[h, i - 1], peer))
            return out

        def start(self, stage):
            go(self.copies(stage))

        def finish(self, stage):
            land(self.copies(stage))
            if stage == 0:
                for h in range(2):
                    for a in range(4):
                        self.q[h, a] = (self.p[h, a, :, c].astype(F32) + self.rc[h, a].astype(F32)).astype(BF16)
            elif stage == 1:
                for h in range(2):
                    total = self.q[h, first_of[h]].astype(F32)
                    for i in range(3):
                        total = total + self.ra[h, i].astype(F32)
                    self.t[h] = total.astype(BF16)

        def result(self):
            halves = []
            for h in range(2):
                total = self.t[h, second_of[h]].astype(F32)
                for i in range(3):
                    total = total + self.rb[h, i].astype(F32)
                halves.append(total)
            return jnp.concatenate(halves, axis=0)

        def drain(self):
            for stage in range(3):
                sent(self.copies(stage))

    m_sum = Sum("m", m_p, m_rc, m_o)
    c_sum = Sum("c", c_p, c_rc, c_o)
    into = Scatter("i", i_p, i_rc, i_q, i_ra, i_t, i_rb)
    outof = Scatter("o", o_p, o_rc, o_q, o_ra, o_t, o_rb)

    def product(t):
        block = dot_nn(wout_ref[:, my_columns], wz[s + t])
        m_p[places(t - 1)] = block.astype(BF16).reshape(4, 2, 16, 128)

    def relay(n, carry):
        odd = 2 * n + 1
        far = 2 * n + 2
        slice_far(s + far).wait_recv()

        @pl.when(s > 1)
        def _():
            slice_far(s + far).start()
            slice_near(s + far).start()

        pl.when(s == 1)(lambda: slice_near(s + far).start())
        slice_near(s + odd).wait_recv()
        product(odd)
        product(far)

        return carry

    steps = (last - s) // 2
    lax.fori_loop(0, steps, relay, 0)

    @pl.when(even)
    def _():
        slice_near(last).wait_recv()
        product(last - s)

    pl.when(wide)(lambda: m_sum.start(0, 0, 2))
    pl.when((~wide) & (s < last))(lambda: m_sum.start(0, 0, 1))

    @pl.when(s <= EARLY)
    def _():
        outof.fill(act_t[...], gl_ref)
        outof.start(0)

    @pl.when(wide)
    def _():
        m_sum.finish(0, 0, 2)
        m_sum.start(1, 0, 2)

    @pl.when(s <= EARLY)
    def _():
        outof.finish(0)
        roots_pack()
        outof.start(1)

    pl.when(wide)(lambda: m_sum.finish(1, 0, 2))

    @pl.when((~wide) & (s < last))
    def _():
        m_sum.finish(0, 0, 1)
        m_sum.start(1, 0, 1)
        m_sum.finish(1, 0, 1)

    @pl.when(~even)
    def _():
        def give(n, carry):
            share_product(last - 1 - s - 2 * n - (1 - c)).start()
            return carry
        lax.fori_loop(0, (last - s) // 2, give, 0)

    pl.when(s > SOON)(lambda: go(roots_first()))

    def cross(index):
        c_p[places(index - s - 1)] = dot_nn(act_t[...], pg[index]).astype(BF16).reshape(4, 2, 16, 128)

    def own_term(index):
        return dot_nt(pg[index], m_o[places(index - s - 1)].reshape(128, 128))

    def next_term(index):
        return dot_nt(pg[index], m_next[index - s - 2].reshape(128, 128))

    lowest = (s + 2) // 2

    @pl.when(even)
    def _():
        land(share_state())

        def come(high, low):
            pass_far(high).wait_recv()
            pass_far(low).wait_recv()

            @pl.when(s > 0)
            def _():
                pass_far(high).start()
                pass_far(low).start()

        def products(high, low):
            share_product(high - s - 2 - c).wait_recv()

        def collect(n, carry):
            high, low = 15 - 2 * n, 14 - 2 * n
            come(high, low)

            @pl.when(s > 0)
            def _():
                pass_near(high).start()
                pass_near(low).start()
            return carry

        def add(n, carry):
            high, low = 15 - 2 * n, 14 - 2 * n
            products(high, low)
            acc_next[...] += next_term(high) + next_term(low)
            acc[...] += own_term(high) + own_term(low)
            return carry

        def spread(n, carry):
            k = last - 2 - s - 2 * n - (1 - c)
            share_product(k).wait_recv()
            pair_product(k).start()
            return carry

        lax.fori_loop(0, 7 - lowest, collect, 0)
        lax.fori_loop(0, 8 - lowest, spread, 0)
        lax.fori_loop(0, 7 - lowest, add, 0)

        @pl.when(s < last - 1)
        def _():
            high, low = 2 * lowest + 1, 2 * lowest
            products(high, low)
            come(high, low)
            pg[s + 1] = ((acc_next[...] + next_term(high) + next_term(low)) * slope_next[...]).astype(BF16)
            pl.when(s > 0)(lambda: pass_far(s + 1).start())
            pg[s] = ((acc[...] + own_term(high) + own_term(low) + own_term(s + 1)) * slope[...]).astype(BF16)

            @pl.when(s > 0)
            def _():
                pass_far(s).start()
                for index in (high, low, s + 1, s):
                    pass_near(index).start()

        @pl.when(s == last - 1)
        def _():
            pg[s + 1] = (acc_next[...] * slope_next[...]).astype(BF16)
            pass_far(s + 1).start()
            pg[s] = ((acc[...] + own_term(s + 1)) * slope[...]).astype(BF16)
            pass_far(s).start()
            pass_near(s + 1).start()
            pass_near(s).start()

    @pl.when(~even)
    def _():
        def collect(n, carry):
            high, low = 15 - 2 * n, 14 - 2 * n
            pass_far(high).wait_recv()
            pass_far(low).wait_recv()
            acc[...] += own_term(high) + own_term(low)
            return carry

        lax.fori_loop(0, 8 - lowest, collect, 0)
        pg[s] = (acc[...] * slope[...]).astype(BF16)

    def cross_two(n, carry):
        cross(s + 1 + 2 * n)
        cross(s + 2 + 2 * n)
        return carry

    lax.fori_loop(0, (last - s) // 2, cross_two, 0)
    pl.when(even)(lambda: cross(last))
    pl.when(wide)(lambda: c_sum.start(0, 0, 2))
    pl.when((~wide) & (s < last))(lambda: c_sum.start(0, 0, 1))

    into.fill(pg[s].astype(F32).T.astype(BF16), x_ref)
    into.start(0)

    into.finish(0)
    into.start(1)

    @pl.when(wide)
    def _():
        c_sum.finish(0, 0, 2)
        c_sum.start(1, 0, 2)

    @pl.when((~wide) & (s < last))
    def _():
        c_sum.finish(0, 0, 1)
        c_sum.start(1, 0, 1)

    @pl.when(s > EARLY)
    def _():
        roots_pack()
        outof.fill(act_t[...], gl_ref)
        outof.start(0)
        outof.finish(0)
        outof.start(1)

    outof.finish(1)
    outof.start(2)
    into.finish(1)
    into.start(2)

    land(roots_second())
    for h in range(2):
        total = r_pk[h, second_of[h]].astype(F32)
        for i in range(3):
            total = total + r_rk[h, i].astype(F32)
        r_sum[h] = total.astype(BF16)
    go(roots_pair())

    def terms(first):
        total = acc_out[...]
        for k in range(first, first + 8):
            total = total + dot_nt(c_o[places(k)].reshape(128, 128), wz[s + 1 + k])
        acc_out[...] = total

    outof.finish(2)
    acc_out[...] = outof.result()

    into.finish(2)
    land(roots_pair())
    for h in range(2):
        merged = (r_sum[h, c].astype(F32) + r_rc[h].astype(F32)).astype(BF16)
        for kind in range(2):
            for what in range(3):
                r_home[kind, what, pl.ds(h * 64, 64)] = merged[kind, what]

    def direct(kind, grad32, out_ref):
        grad = grad32.astype(BF16)
        exact = grad.astype(F32)
        first = dot_nn(r_home[kind, 0], grad)
        high = first.astype(BF16)
        low = (first - high.astype(F32)).astype(BF16)
        right = r_home[kind, 1]
        precond = dot_nn(high, right) + dot_nn(low, right)
        grad_sq = jnp.sum(jnp.sum(exact * exact, axis=1, keepdims=True), axis=0, keepdims=True)
        pre_sq = jnp.sum(jnp.sum(precond * precond, axis=1, keepdims=True), axis=0, keepdims=True)
        direction = precond * (jnp.sqrt(grad_sq) * lax.rsqrt(pre_sq + 1e-06))
        out_ref[...] = (MOMENTUM_DECAY * r_home[kind, 2].astype(F32) + direction).astype(BF16)
        rounded = direction.astype(BF16)
        for h in range(2):
            d_x[h, first_of[h], c, kind] = rounded[h * 64:(h + 1) * 64]

    direct(0, into.result().T * (1.0 / 32), search_in_ref)

    def way_first(kind):
        copies = []
        for h in range(2):
            mine = d_x.at[h, first_of[h], c, kind]
            for i in range(1, 4):
                copies.append(remote(("da", h, i, kind), mine, mine, peer_first(h, i)[1]))
        return copies

    go(way_first(0))

    @pl.when(wide)
    def _():
        c_sum.finish(1, 0, 2)
        terms(8)
        terms(0)

    @pl.when((~wide) & (s < last))
    def _():
        c_sum.finish(1, 0, 1)
        terms(0)

    direct(1, acc_out[...] * (1.0 / 32), search_out_ref)

    def way_pair():
        mine = d_x.at[:, :, c]
        return [remote(("dc",), mine, mine, sibling)]

    def way_second():
        copies = []
        for h in range(2):
            for i in range(1, 4):
                b, peer = peer_second(h, i)
                copies.append(remote(("db", h, i), d_pk.at[h, b], d_rk.at[h, i - 1], peer))
        return copies

    go(way_first(1))
    land(way_first(0))
    land(way_first(1))
    go(way_pair())
    land(way_pair())
    for h in range(2):
        def slot(t, carry):
            b, k = t // 4, lax.rem(t, 4)
            owner = device(h, first_of[h], b)
            block = lists_ref[0, k, owner]
            kind = block // 32
            hx, hy, core = lax.rem(block // 8, 4), lax.rem(block // 2, 4), lax.rem(block, 2)
            a, row = (hx, hy) if h == 0 else (hy, hx)
            here = (row == second_of[h]) & (count_ref[0, owner] > k)
            value = d_x[h, a, core, kind]
            d_pk[h, b, k] = jnp.where(here, value, jnp.zeros_like(value))
            return carry
        lax.fori_loop(0, 16, slot, 0)
    go(way_second())
    land(way_second())
    for h in range(2):
        total = d_pk[h, second_of[h]].astype(F32)
        for i in range(3):
            total = total + d_rk[h, i].astype(F32)
        rows = pl.ds(h * 64, 64)
        for k in range(4):
            old = mom_ref[k, rows]
            new = MOMENTUM_DECAY * old + total[k]
            newmom_ref[k, rows] = jnp.where(count_ref[0, dp] > k, new, old)

    pl.when(s > 1)(lambda: own_far().wait_send())
    pl.when(s > 0)(lambda: own_near().wait_send())

    def leave(t, carry):
        @pl.when(lax.rem(t, 2) == 0)
        def _():
            pl.when(s > 1)(lambda: slice_far(s + t).wait_send())
            pl.when(s > 0)(lambda: slice_near(s + t).wait_send())
        return carry

    lax.fori_loop(1, sections - s, leave, 0)

    @pl.when(even & (s > 0))
    def _():
        def passed(index, carry):
            pass_far(index).wait_send()
            pass_near(index).wait_send()
            return carry
        lax.fori_loop(s, sections, passed, 0)

    @pl.when(~even)
    def _():
        sent(share_state())

        def given(n, carry):
            share_product(last - 1 - s - 2 * n - (1 - c)).wait_send()
            return carry
        lax.fori_loop(0, (last - s) // 2, given, 0)

    @pl.when(even)
    def _():
        def given_pair(n, carry):
            pair_product(last - 2 - s - 2 * n - (1 - c)).wait_send()
            return carry
        lax.fori_loop(0, 8 - lowest, given_pair, 0)

    @pl.when(wide)
    def _():
        m_sum.drain(0, 2)
        c_sum.drain(0, 2)

    @pl.when((~wide) & (s < last))
    def _():
        m_sum.drain(0, 1)
        c_sum.drain(0, 1)

    into.drain()
    outof.drain()
    sent(roots_first())
    sent(roots_second())
    sent(roots_pair())
    sent(way_first(0))
    sent(way_first(1))
    sent(way_pair())
    sent(way_second())


def on_device(
    sections, saved_inputs, loss_grad, w_in, w_out, left_root, right_root, momentum, owned_blocks, owned_count
):
    vmem = pl.BlockSpec(memory_space=pltpu.VMEM)
    hbm = pl.BlockSpec(memory_space=pltpu.HBM)
    smem = pl.BlockSpec(memory_space=pltpu.SMEM)

    def room(*shape, kind=BF16):
        return pltpu.VMEM(shape, kind)

    def sum_room():
        return [
            room(2, 2, 4, 4, 2, 16, 128), room(31, 2, 2, 16, 128), room(2, 2, 4, 4, 2, 16, 128),
        ]

    def scatter_room():
        return [
            room(2, 4, 4, 2, 64, 128), room(2, 4, 4, 64, 128), room(2, 4, 4, 64, 128),
            room(2, 3, 4, 64, 128), room(2, 4, 64, 128), room(2, 3, 64, 128),
        ]

    scratch = (
        [
            room(128, 4096), room(128, 4096), room(4096, 128), room(128, 4096), room(4, 128, 128, kind=F32),
            room(sections + 8, 128, 128), room(sections, 128, 128),
            room(128, 128, kind=F32), room(128, 128, kind=F32), room(128, 128, kind=F32), room(128, 128, kind=F32), room(128, 128),
            room(128, 128, kind=F32), room(128, 128, kind=F32), room(16, 4, 2, 16, 128),
        ]
        + sum_room() + sum_room() + scatter_room() + scatter_room()
        + [
            room(2, 16, 3, 64, 128), room(2, 4, 2, 2, 3, 64, 128), room(2, 3, 2, 2, 3, 64, 128),
            room(2, 2, 2, 3, 64, 128), room(2, 2, 3, 64, 128), room(2, 3, 128, 128),
            room(2, 4, 2, 2, 64, 128), room(2, 4, 4, 64, 128), room(2, 3, 4, 64, 128),
        ]
        + [pltpu.SemaphoreType.DMA((9,))]
        + [pltpu.SemaphoreType.DMA((COPIES,))] * 2
        + [pltpu.SemaphoreType.DMA((sections,))] * 8
        + [pltpu.SemaphoreType.DMA((2,))] * 2
    )
    new_mom, search_in, search_out = pl.pallas_call(
        functools.partial(kernel, sections),
        out_shape=(
            jax.ShapeDtypeStruct((4, 128, 128), F32),
            jax.ShapeDtypeStruct((128, 128), BF16),
            jax.ShapeDtypeStruct((128, 128), BF16),
        ),
        in_specs=[hbm] * 7 + [smem] * 2,
        out_specs=(vmem, vmem, vmem),
        scratch_shapes=scratch,
        compiler_params=pltpu.CompilerParams(
            collective_id=0, has_side_effects=True, vmem_limit_bytes=60 * 1024 * 1024
        ),
        name="drain",
    )(
        saved_inputs.reshape(128, 4096), loss_grad.reshape(128, 4096), w_in[0], w_out[0],
        left_root[0, 0], right_root[0, 0], momentum[0, 0],
        jnp.swapaxes(owned_blocks, 1, 2), owned_count,
    )
    return new_mom[None, None], search_in[None], search_out[None]


def solution(mesh):
    placed = (
        P("section", None, "dp", None),
        P(None, "dp", None),
        P("section", None, None),
        P("section", None, None),
        P("section", "dp", None, None, None),
        P("section", "dp", None, None, None),
        P("section", "dp", None, None, None),
        P("section", None, None),
        P("section", None),
    )
    return jax.shard_map(
        functools.partial(on_device, mesh.shape["section"]),
        mesh=mesh,
        in_specs=placed,
        out_specs=(
            P("section", "dp", None, None, None),
            P("section", "dp", None),
            P("section", None, "dp"),
        ),
        check_vma=False,
    )
```

```python
import functools

import jax
import jax.numpy as jnp
from jax import lax
from jax.experimental import pallas as pl
from jax.experimental.pallas import tpu as pltpu
from jax.sharding import PartitionSpec as P

MOMENTUM_DECAY = 0.9
MESH = pl.DeviceIdType.MESH
BF16 = jnp.bfloat16
F32 = jnp.float32
COPIES = 72
EARLY = 3
SOON = 8


def dot_nn(a, b):
    return lax.dot_general(a, b, (((1,), (0,)), ((), ())), preferred_element_type=F32)


def dot_nt(a, b):
    return lax.dot_general(a, b, (((1,), (1,)), ((), ())), preferred_element_type=F32)


def silu_slope(values):
    sigma = jax.nn.sigmoid(values)
    return sigma * (1.0 + values * (1.0 - sigma))


def kernel(
    sections,
    x_hbm, gl_hbm, win_hbm, wout_hbm, left_hbm, right_hbm, mom_hbm, lists_ref, count_ref,
    newmom_ref, search_in_ref, search_out_ref,
    x_ref, gl_ref, win_ref, wout_ref, mom_ref,
    wz, pg, slope, base, acc, acc_out, act_t, slope_next, acc_next, m_next,
    m_p, m_pc, m_q, m_rc, m_o,
    c_p, c_pc, c_q, c_rc, c_o,
    i_p, i_rc, i_q, i_ra, i_t, i_rb,
    o_p, o_rc, o_q, o_ra, o_t, o_rb,
    r_x, r_pk, r_rk, r_sum, r_rc, r_home,
    d_x, d_pk, d_rk,
    local, send, recv, z_near, z_far, z_recv, p_near, p_far, p_recv, n_send, n_recv, b_send, b_recv,
):
    s = lax.axis_index("section")
    dp = lax.axis_index("dp")
    c = lax.rem(dp, 2)
    y = lax.rem(dp // 2, 4)
    x = dp // 8
    last = sections - 1
    first_of = (x, y)
    second_of = (y, x)
    wide = s <= last - 9
    ids = {}

    def sid(key):
        return ids.setdefault(key, len(ids))

    def device(h, a, b):
        return (a * 4 + b) * 2 + c if h == 0 else (b * 4 + a) * 2 + c

    def remote(key, source, target, peer):
        number = sid(key)
        return pltpu.make_async_remote_copy(
            src_ref=source, dst_ref=target, send_sem=send.at[number], recv_sem=recv.at[number],
            device_id={"dp": peer}, device_id_type=MESH,
        )

    sibling = dp + 1 - 2 * c

    def peer_first(h, i):
        a = lax.rem(first_of[h] + i, 4)
        return a, device(h, a, second_of[h])

    def peer_second(h, i):
        b = lax.rem(second_of[h] + i, 4)
        return b, device(h, first_of[h], b)

    def go(copies):
        for copy in copies:
            copy.start()

    def land(copies):
        for copy in copies:
            copy.wait_recv()

    def sent(copies):
        for copy in copies:
            copy.wait_send()

    barrier = pltpu.get_barrier_semaphore()

    def greet(i, carry):
        pl.semaphore_signal(barrier, inc=1, device_id={"dp": lax.rem(dp + 2 * i, 32)}, device_id_type=MESH)
        return carry

    lax.fori_loop(1, 16, greet, 0)
    pl.semaphore_signal(barrier, inc=1, device_id={"dp": sibling}, device_id_type=MESH)
    below = lax.rem(s + last, sections)
    below_two = lax.rem(s + last - 1, sections)
    even = lax.rem(s, 2) == 0
    for peer in (below, below_two, lax.rem(s + 1, sections), lax.rem(s + 2, sections)):
        pl.semaphore_signal(barrier, inc=1, device_id={"section": peer}, device_id_type=MESH)

    fetches = {}

    def fetch(name, source, target):
        fetches[name] = pltpu.make_async_copy(source, target, local.at[len(fetches)])
        fetches[name].start()

    fetch("x", x_hbm, x_ref)
    fetch("win", win_hbm, win_ref)
    fetch("gl", gl_hbm, gl_ref)
    fetch("wout", wout_hbm, wout_ref)
    fetch("mom", mom_hbm, mom_ref)
    for h in range(2):
        rows = pl.ds(h * 64, 64)
        slots = pl.ds(first_of[h] * 4, 4)
        fetch(("left", h), left_hbm.at[:, rows], r_x.at[h, slots, 0])
        fetch(("right", h), right_hbm.at[:, rows], r_x.at[h, slots, 1])

    pl.semaphore_wait(barrier, 20)

    def to_section(source, target, send_sem, recv_sem, peer):
        return pltpu.make_async_remote_copy(
            src_ref=source, dst_ref=target, send_sem=send_sem, recv_sem=recv_sem,
            device_id={"section": peer}, device_id_type=MESH,
        )

    def slice_near(index):
        return to_section(wz.at[index], wz.at[index], z_near.at[index], z_recv.at[index], below)

    def slice_far(index):
        return to_section(wz.at[index], wz.at[index], z_far.at[index], z_recv.at[index], below_two)

    my_columns = pl.ds(pl.multiple_of(dp * 128, 128), 128)

    def own_near():
        return to_section(win_hbm.at[my_columns], wz.at[s], z_near.at[s], z_recv.at[s], below)

    def own_far():
        return to_section(win_hbm.at[my_columns], wz.at[s], z_far.at[s], z_recv.at[s], below_two)

    def pass_near(index):
        return to_section(pg.at[index], pg.at[index], p_near.at[index], p_recv.at[index], below)

    def pass_far(index):
        return to_section(pg.at[index], pg.at[index], p_far.at[index], p_recv.at[index], below_two)

    def share_state():
        return [
            to_section(base, acc_next, b_send.at[0], b_recv.at[0], below),
            to_section(slope, slope_next, b_send.at[1], b_recv.at[1], below),
        ]

    def places(k):
        if isinstance(k, int):
            return k // 8, k // 4 % 2, k % 4
        return k // 8, lax.rem(k // 4, 2), lax.rem(k, 4)

    def share_product(k):
        return to_section(m_o.at[places(k)], m_next.at[k], n_send.at[k], n_recv.at[k], below)

    def pair_product(k):
        return pltpu.make_async_remote_copy(
            src_ref=m_next.at[k], dst_ref=m_next.at[k], send_sem=n_send.at[k], recv_sem=n_recv.at[k],
            device_id={"dp": sibling}, device_id_type=MESH,
        )

    pl.when(s > 1)(lambda: own_far().start())
    pl.when(s > 0)(lambda: own_near().start())

    def roots_first():
        copies = []
        for h in range(2):
            mine = r_x.at[h, pl.ds(first_of[h] * 4, 4)]
            for i in range(1, 4):
                copies.append(remote(("ra", h, i), mine, mine, peer_first(h, i)[1]))
        return copies

    def roots_second():
        copies = []
        for h in range(2):
            for i in range(1, 4):
                b, peer = peer_second(h, i)
                copies.append(remote(("rb", h, i), r_pk.at[h, b], r_rk.at[h, i - 1], peer))
        return copies

    def roots_pair():
        return [remote(("rc",), r_sum.at[:, 1 - c], r_rc, sibling)]

    def roots_pack():
        land(roots_first())
        for h in range(2):
            def target(t, carry):
                b, core, kind = t // 4, lax.rem(t // 2, 2), lax.rem(t, 2)
                if h == 0:
                    place = (first_of[h] * 4 + b) * 2 + core
                else:
                    place = (b * 4 + first_of[h]) * 2 + core
                block = kind * 32 + place
                index = jnp.int32(0)
                found = jnp.int32(0)
                for a in range(4):
                    owner = device(h, a, second_of[h])
                    held = count_ref[0, owner]
                    for k in range(4):
                        hit = (lists_ref[0, k, owner] == block) & (held > k)
                        index = index + jnp.where(hit, a * 4 + k, 0)
                        found = found + jnp.where(hit, 1, 0)
                value = r_x[h, index]
                r_pk[h, b, core, kind] = jnp.where(found > 0, value, jnp.zeros_like(value))
                return carry
            lax.fori_loop(0, 16, target, 0)
        go(roots_second())

    fetches["x"].wait()
    fetches["win"].wait()
    pre = dot_nn(x_ref[...], win_ref[...])
    slope[...] = silu_slope(pre)
    act = jax.nn.silu(pre)
    act_t[...] = act.T.astype(BF16)
    fetches["gl"].wait()
    fetches["wout"].wait()
    base[...] = dot_nt(gl_ref[...], wout_ref[...])
    acc[...] = base[...]

    @pl.when(~even)
    def _():
        go(share_state())

    fetches["mom"].wait()
    for h in range(2):
        for k in range(4):
            r_x[h, first_of[h] * 4 + k, 2] = mom_ref[k, pl.ds(h * 64, 64)].astype(BF16)
        fetches[("left", h)].wait()
        fetches[("right", h)].wait()

    @pl.when(s <= SOON)
    def _():
        go(roots_first())

    wz[sections:] = jnp.zeros_like(wz[sections:])
    m_p[...] = jnp.zeros_like(m_p)
    c_p[...] = jnp.zeros_like(c_p)

    class Sum:
        def __init__(self, name, p, pc, q, rc, o):
            self.name, self.p, self.pc, self.q, self.rc, self.o = name, p, pc, q, rc, o

        def pair(self, stage, first, size):
            part = pl.ds(first, size)
            if stage == 0:
                return [remote((self.name, "pair", 0), self.p.at[part, :, :, :, 1 - c], self.pc.at[part], sibling)]
            mine = self.o.at[part, :, :, :, c]
            return [remote((self.name, "pair", 1), mine, mine, sibling)]

        def start(self, stage, first, size):
            number = sid((self.name, stage, first))
            part = pl.ds(first, size)
            if stage == 0:
                go(self.pair(0, first, size))
                land(self.pair(0, first, size))
                for chunk in range(first, first + size):
                    for h in range(2):
                        both = self.p[chunk, h, :, :, c].astype(F32) + self.pc[chunk, h].astype(F32)
                        self.q[chunk, h] = both.astype(BF16)

            def one(i, carry):
                peer = lax.rem(dp + 2 * i, 32)
                if stage == 0:
                    source = self.q.at[part, :, peer // 8, lax.rem(peer // 2, 4)]
                    target = self.rc.at[i - 1, part]
                else:
                    source = target = self.o.at[part, :, x, y, c]
                pltpu.make_async_remote_copy(
                    src_ref=source, dst_ref=target, send_sem=send.at[number], recv_sem=recv.at[number],
                    device_id={"dp": peer}, device_id_type=MESH,
                ).start()
                return carry

            lax.fori_loop(1, 16, one, 0)

        def all_bytes(self, sems, stage, first, size):
            number = sid((self.name, stage, first))
            every = self.rc.at[:, pl.ds(first, size)]
            pltpu.make_async_copy(every, every, sems.at[number]).wait()

        def finish(self, stage, first, size):
            self.all_bytes(recv, stage, first, size)
            if stage == 0:
                part = pl.ds(first, size)
                total = self.q[part, :, x, y].astype(F32)
                for i in range(15):
                    total = total + self.rc[i, part].astype(F32)
                self.o[part, :, x, y, c] = total.astype(BF16)
            else:
                go(self.pair(1, first, size))
                land(self.pair(1, first, size))

        def drain(self, first, size):
            for stage in range(2):
                self.all_bytes(send, stage, first, size)
                sent(self.pair(stage, first, size))

    class Scatter:
        def __init__(self, name, p, rc, q, ra, t, rb):
            self.name, self.p, self.rc, self.q = name, p, rc, q
            self.ra, self.t, self.rb = ra, t, rb

        def fill(self, left, right_ref):
            def chip(n, carry):
                cx, cy = n // 4, lax.rem(n, 4)
                columns = pl.ds(pl.multiple_of(n * 256, 256), 256)
                product = dot_nn(left, right_ref[:, columns]).astype(BF16)
                for core in range(2):
                    block = product[:, core * 128:(core + 1) * 128]
                    self.p[0, cx, cy, core] = block[:64]
                    self.p[1, cy, cx, core] = block[64:]
                return carry
            lax.fori_loop(0, 16, chip, 0)

        def copies(self, stage):
            n = self.name
            if stage == 0:
                return [remote((n, 0), self.p.at[:, :, :, 1 - c], self.rc, sibling)]
            out = []
            for h in range(2):
                for i in range(1, 4):
                    if stage == 1:
                        a, peer = peer_first(h, i)
                        out.append(remote((n, 1, h, i), self.q.at[h, a], self.ra.at[h, i - 1], peer))
                    else:
                        b, peer = peer_second(h, i)
                        out.append(remote((n, 2, h, i), self.t.at[h, b], self.rb.at[h, i - 1], peer))
            return out

        def start(self, stage):
            go(self.copies(stage))

        def finish(self, stage):
            land(self.copies(stage))
            if stage == 0:
                for h in range(2):
                    for a in range(4):
                        self.q[h, a] = (self.p[h, a, :, c].astype(F32) + self.rc[h, a].astype(F32)).astype(BF16)
            elif stage == 1:
                for h in range(2):
                    total = self.q[h, first_of[h]].astype(F32)
                    for i in range(3):
                        total = total + self.ra[h, i].astype(F32)
                    self.t[h] = total.astype(BF16)

        def result(self):
            halves = []
            for h in range(2):
                total = self.t[h, second_of[h]].astype(F32)
                for i in range(3):
                    total = total + self.rb[h, i].astype(F32)
                halves.append(total)
            return jnp.concatenate(halves, axis=0)

        def drain(self):
            for stage in range(3):
                sent(self.copies(stage))

    m_sum = Sum("m", m_p, m_pc, m_q, m_rc, m_o)
    c_sum = Sum("c", c_p, c_pc, c_q, c_rc, c_o)
    into = Scatter("i", i_p, i_rc, i_q, i_ra, i_t, i_rb)
    outof = Scatter("o", o_p, o_rc, o_q, o_ra, o_t, o_rb)

    def product(t):
        block = dot_nn(wout_ref[:, my_columns], wz[s + t])
        m_p[places(t - 1)] = block.astype(BF16).reshape(4, 2, 16, 128)

    def relay(n, carry):
        odd = 2 * n + 1
        far = 2 * n + 2
        slice_far(s + far).wait_recv()

        @pl.when(s > 1)
        def _():
            slice_far(s + far).start()
            slice_near(s + far).start()

        pl.when(s == 1)(lambda: slice_near(s + far).start())
        slice_near(s + odd).wait_recv()
        product(odd)
        product(far)

        return carry

    steps = (last - s) // 2
    lax.fori_loop(0, steps, relay, 0)

    @pl.when(even)
    def _():
        slice_near(last).wait_recv()
        product(last - s)

    pl.when(wide)(lambda: m_sum.start(0, 0, 2))
    pl.when((~wide) & (s < last))(lambda: m_sum.start(0, 0, 1))

    @pl.when(s <= EARLY)
    def _():
        outof.fill(act_t[...], gl_ref)
        outof.start(0)

    @pl.when(wide)
    def _():
        m_sum.finish(0, 0, 2)
        m_sum.start(1, 0, 2)

    @pl.when(s <= EARLY)
    def _():
        outof.finish(0)
        roots_pack()
        outof.start(1)

    pl.when(wide)(lambda: m_sum.finish(1, 0, 2))

    @pl.when((~wide) & (s < last))
    def _():
        m_sum.finish(0, 0, 1)
        m_sum.start(1, 0, 1)
        m_sum.finish(1, 0, 1)

    @pl.when(~even)
    def _():
        def give(n, carry):
            share_product(last - 1 - s - 2 * n - (1 - c)).start()
            return carry
        lax.fori_loop(0, (last - s) // 2, give, 0)

    pl.when(s > SOON)(lambda: go(roots_first()))

    def cross(index):
        c_p[places(index - s - 1)] = dot_nn(act_t[...], pg[index]).astype(BF16).reshape(4, 2, 16, 128)

    def own_term(index):
        return dot_nt(pg[index], m_o[places(index - s - 1)].reshape(128, 128))

    def next_term(index):
        return dot_nt(pg[index], m_next[index - s - 2].reshape(128, 128))

    lowest = (s + 2) // 2

    @pl.when(even)
    def _():
        land(share_state())

        def come(high, low):
            pass_far(high).wait_recv()
            pass_far(low).wait_recv()

            @pl.when(s > 0)
            def _():
                pass_far(high).start()
                pass_far(low).start()

        def products(high, low):
            share_product(high - s - 2 - c).wait_recv()

        def collect(n, carry):
            high, low = 15 - 2 * n, 14 - 2 * n
            come(high, low)

            @pl.when(s > 0)
            def _():
                pass_near(high).start()
                pass_near(low).start()
            return carry

        def add(n, carry):
            high, low = 15 - 2 * n, 14 - 2 * n
            products(high, low)
            acc_next[...] += next_term(high) + next_term(low)
            acc[...] += own_term(high) + own_term(low)
            return carry

        def spread(n, carry):
            k = last - 2 - s - 2 * n - (1 - c)
            share_product(k).wait_recv()
            pair_product(k).start()
            return carry

        lax.fori_loop(0, 7 - lowest, collect, 0)
        lax.fori_loop(0, 8 - lowest, spread, 0)
        lax.fori_loop(0, 7 - lowest, add, 0)

        @pl.when(s < last - 1)
        def _():
            high, low = 2 * lowest + 1, 2 * lowest
            products(high, low)
            come(high, low)
            pg[s + 1] = ((acc_next[...] + next_term(high) + next_term(low)) * slope_next[...]).astype(BF16)
            pl.when(s > 0)(lambda: pass_far(s + 1).start())
            pg[s] = ((acc[...] + own_term(high) + own_term(low) + own_term(s + 1)) * slope[...]).astype(BF16)

            @pl.when(s > 0)
            def _():
                pass_far(s).start()
                for index in (high, low, s + 1, s):
                    pass_near(index).start()

        @pl.when(s == last - 1)
        def _():
            pg[s + 1] = (acc_next[...] * slope_next[...]).astype(BF16)
            pass_far(s + 1).start()
            pg[s] = ((acc[...] + own_term(s + 1)) * slope[...]).astype(BF16)
            pass_far(s).start()
            pass_near(s + 1).start()
            pass_near(s).start()

    @pl.when(~even)
    def _():
        def collect(n, carry):
            high, low = 15 - 2 * n, 14 - 2 * n
            pass_far(high).wait_recv()
            pass_far(low).wait_recv()
            acc[...] += own_term(high) + own_term(low)
            return carry

        lax.fori_loop(0, 8 - lowest, collect, 0)
        pg[s] = (acc[...] * slope[...]).astype(BF16)

    def cross_two(n, carry):
        cross(s + 1 + 2 * n)
        cross(s + 2 + 2 * n)
        return carry

    lax.fori_loop(0, (last - s) // 2, cross_two, 0)
    pl.when(even)(lambda: cross(last))
    pl.when(wide)(lambda: c_sum.start(0, 0, 2))
    pl.when((~wide) & (s < last))(lambda: c_sum.start(0, 0, 1))

    into.fill(pg[s].astype(F32).T.astype(BF16), x_ref)
    into.start(0)

    into.finish(0)
    into.start(1)

    @pl.when(wide)
    def _():
        c_sum.finish(0, 0, 2)
        c_sum.start(1, 0, 2)

    @pl.when((~wide) & (s < last))
    def _():
        c_sum.finish(0, 0, 1)
        c_sum.start(1, 0, 1)

    @pl.when(s > EARLY)
    def _():
        roots_pack()
        outof.fill(act_t[...], gl_ref)
        outof.start(0)
        outof.finish(0)
        outof.start(1)

    outof.finish(1)
    outof.start(2)
    into.finish(1)
    into.start(2)

    land(roots_second())
    for h in range(2):
        total = r_pk[h, second_of[h]].astype(F32)
        for i in range(3):
            total = total + r_rk[h, i].astype(F32)
        r_sum[h] = total.astype(BF16)
    go(roots_pair())

    def terms(first):
        total = acc_out[...]
        for k in range(first, first + 8):
            total = total + dot_nt(c_o[places(k)].reshape(128, 128), wz[s + 1 + k])
        acc_out[...] = total

    outof.finish(2)
    acc_out[...] = outof.result()

    into.finish(2)
    land(roots_pair())
    for h in range(2):
        merged = (r_sum[h, c].astype(F32) + r_rc[h].astype(F32)).astype(BF16)
        for kind in range(2):
            for what in range(3):
                r_home[kind, what, pl.ds(h * 64, 64)] = merged[kind, what]

    def direct(kind, grad32, out_ref):
        grad = grad32.astype(BF16)
        exact = grad.astype(F32)
        first = dot_nn(r_home[kind, 0], grad)
        high = first.astype(BF16)
        low = (first - high.astype(F32)).astype(BF16)
        right = r_home[kind, 1]
        precond = dot_nn(high, right) + dot_nn(low, right)
        grad_sq = jnp.sum(jnp.sum(exact * exact, axis=1, keepdims=True), axis=0, keepdims=True)
        pre_sq = jnp.sum(jnp.sum(precond * precond, axis=1, keepdims=True), axis=0, keepdims=True)
        direction = precond * (jnp.sqrt(grad_sq) * lax.rsqrt(pre_sq + 1e-06))
        out_ref[...] = (MOMENTUM_DECAY * r_home[kind, 2].astype(F32) + direction).astype(BF16)
        rounded = direction.astype(BF16)
        for h in range(2):
            d_x[h, first_of[h], c, kind] = rounded[h * 64:(h + 1) * 64]

    direct(0, into.result().T * (1.0 / 32), search_in_ref)

    def way_first(kind):
        copies = []
        for h in range(2):
            mine = d_x.at[h, first_of[h], c, kind]
            for i in range(1, 4):
                copies.append(remote(("da", h, i, kind), mine, mine, peer_first(h, i)[1]))
        return copies

    go(way_first(0))

    @pl.when(wide)
    def _():
        c_sum.finish(1, 0, 2)
        terms(8)
        terms(0)

    @pl.when((~wide) & (s < last))
    def _():
        c_sum.finish(1, 0, 1)
        terms(0)

    direct(1, acc_out[...] * (1.0 / 32), search_out_ref)

    def way_pair():
        mine = d_x.at[:, :, c]
        return [remote(("dc",), mine, mine, sibling)]

    def way_second():
        copies = []
        for h in range(2):
            for i in range(1, 4):
                b, peer = peer_second(h, i)
                copies.append(remote(("db", h, i), d_pk.at[h, b], d_rk.at[h, i - 1], peer))
        return copies

    go(way_first(1))
    land(way_first(0))
    land(way_first(1))
    go(way_pair())
    land(way_pair())
    for h in range(2):
        def slot(t, carry):
            b, k = t // 4, lax.rem(t, 4)
            owner = device(h, first_of[h], b)
            block = lists_ref[0, k, owner]
            kind = block // 32
            hx, hy, core = lax.rem(block // 8, 4), lax.rem(block // 2, 4), lax.rem(block, 2)
            a, row = (hx, hy) if h == 0 else (hy, hx)
            here = (row == second_of[h]) & (count_ref[0, owner] > k)
            value = d_x[h, a, core, kind]
            d_pk[h, b, k] = jnp.where(here, value, jnp.zeros_like(value))
            return carry
        lax.fori_loop(0, 16, slot, 0)
    go(way_second())
    land(way_second())
    for h in range(2):
        total = d_pk[h, second_of[h]].astype(F32)
        for i in range(3):
            total = total + d_rk[h, i].astype(F32)
        rows = pl.ds(h * 64, 64)
        for k in range(4):
            old = mom_ref[k, rows]
            new = MOMENTUM_DECAY * old + total[k]
            newmom_ref[k, rows] = jnp.where(count_ref[0, dp] > k, new, old)

    pl.when(s > 1)(lambda: own_far().wait_send())
    pl.when(s > 0)(lambda: own_near().wait_send())

    def leave(t, carry):
        @pl.when(lax.rem(t, 2) == 0)
        def _():
            pl.when(s > 1)(lambda: slice_far(s + t).wait_send())
            pl.when(s > 0)(lambda: slice_near(s + t).wait_send())
        return carry

    lax.fori_loop(1, sections - s, leave, 0)

    @pl.when(even & (s > 0))
    def _():
        def passed(index, carry):
            pass_far(index).wait_send()
            pass_near(index).wait_send()
            return carry
        lax.fori_loop(s, sections, passed, 0)

    @pl.when(~even)
    def _():
        sent(share_state())

        def given(n, carry):
            share_product(last - 1 - s - 2 * n - (1 - c)).wait_send()
            return carry
        lax.fori_loop(0, (last - s) // 2, given, 0)

    @pl.when(even)
    def _():
        def given_pair(n, carry):
            pair_product(last - 2 - s - 2 * n - (1 - c)).wait_send()
            return carry
        lax.fori_loop(0, 8 - lowest, given_pair, 0)

    @pl.when(wide)
    def _():
        m_sum.drain(0, 2)
        c_sum.drain(0, 2)

    @pl.when((~wide) & (s < last))
    def _():
        m_sum.drain(0, 1)
        c_sum.drain(0, 1)

    into.drain()
    outof.drain()
    sent(roots_first())
    sent(roots_second())
    sent(roots_pair())
    sent(way_first(0))
    sent(way_first(1))
    sent(way_pair())
    sent(way_second())


def on_device(
    sections, saved_inputs, loss_grad, w_in, w_out, left_root, right_root, momentum, owned_blocks, owned_count
):
    vmem = pl.BlockSpec(memory_space=pltpu.VMEM)
    hbm = pl.BlockSpec(memory_space=pltpu.HBM)
    smem = pl.BlockSpec(memory_space=pltpu.SMEM)

    def room(*shape, kind=BF16):
        return pltpu.VMEM(shape, kind)

    def sum_room():
        return [
            room(2, 2, 4, 4, 2, 16, 128), room(2, 2, 4, 4, 16, 128), room(2, 2, 4, 4, 16, 128), room(15, 2, 2, 16, 128), room(2, 2, 4, 4, 2, 16, 128),
        ]

    def scatter_room():
        return [
            room(2, 4, 4, 2, 64, 128), room(2, 4, 4, 64, 128), room(2, 4, 4, 64, 128),
            room(2, 3, 4, 64, 128), room(2, 4, 64, 128), room(2, 3, 64, 128),
        ]

    scratch = (
        [
            room(128, 4096), room(128, 4096), room(4096, 128), room(128, 4096), room(4, 128, 128, kind=F32),
            room(sections + 8, 128, 128), room(sections, 128, 128),
            room(128, 128, kind=F32), room(128, 128, kind=F32), room(128, 128, kind=F32), room(128, 128, kind=F32), room(128, 128),
            room(128, 128, kind=F32), room(128, 128, kind=F32), room(16, 4, 2, 16, 128),
        ]
        + sum_room() + sum_room() + scatter_room() + scatter_room()
        + [
            room(2, 16, 3, 64, 128), room(2, 4, 2, 2, 3, 64, 128), room(2, 3, 2, 2, 3, 64, 128),
            room(2, 2, 2, 3, 64, 128), room(2, 2, 3, 64, 128), room(2, 3, 128, 128),
            room(2, 4, 2, 2, 64, 128), room(2, 4, 4, 64, 128), room(2, 3, 4, 64, 128),
        ]
        + [pltpu.SemaphoreType.DMA((9,))]
        + [pltpu.SemaphoreType.DMA((COPIES,))] * 2
        + [pltpu.SemaphoreType.DMA((sections,))] * 8
        + [pltpu.SemaphoreType.DMA((2,))] * 2
    )
    new_mom, search_in, search_out = pl.pallas_call(
        functools.partial(kernel, sections),
        out_shape=(
            jax.ShapeDtypeStruct((4, 128, 128), F32),
            jax.ShapeDtypeStruct((128, 128), BF16),
            jax.ShapeDtypeStruct((128, 128), BF16),
        ),
        in_specs=[hbm] * 7 + [smem] * 2,
        out_specs=(vmem, vmem, vmem),
        scratch_shapes=scratch,
        compiler_params=pltpu.CompilerParams(
            collective_id=0, has_side_effects=True, vmem_limit_bytes=60 * 1024 * 1024
        ),
        name="drain",
    )(
        saved_inputs.reshape(128, 4096), loss_grad.reshape(128, 4096), w_in[0], w_out[0],
        left_root[0, 0], right_root[0, 0], momentum[0, 0],
        jnp.swapaxes(owned_blocks, 1, 2), owned_count,
    )
    return new_mom[None, None], search_in[None], search_out[None]


def solution(mesh):
    placed = (
        P("section", None, "dp", None),
        P(None, "dp", None),
        P("section", None, None),
        P("section", None, None),
        P("section", "dp", None, None, None),
        P("section", "dp", None, None, None),
        P("section", "dp", None, None, None),
        P("section", None, None),
        P("section", None),
    )
    return jax.shard_map(
        functools.partial(on_device, mesh.shape["section"]),
        mesh=mesh,
        in_specs=placed,
        out_specs=(
            P("section", "dp", None, None, None),
            P("section", "dp", None),
            P("section", None, "dp"),
        ),
        check_vma=False,
    )
```

```python
import functools

import jax
import jax.numpy as jnp
from jax import lax
from jax.experimental import pallas as pl
from jax.experimental.pallas import tpu as pltpu
from jax.sharding import PartitionSpec as P

MOMENTUM_DECAY = 0.9
MESH = pl.DeviceIdType.MESH
BF16 = jnp.bfloat16
F32 = jnp.float32
COPIES = 72
EARLY = 3
SOON = 8


def dot_nn(a, b):
    return lax.dot_general(a, b, (((1,), (0,)), ((), ())), preferred_element_type=F32)


def dot_nt(a, b):
    return lax.dot_general(a, b, (((1,), (1,)), ((), ())), preferred_element_type=F32)


def silu_slope(values):
    sigma = jax.nn.sigmoid(values)
    return sigma * (1.0 + values * (1.0 - sigma))


def kernel(
    sections,
    x_hbm, gl_hbm, win_hbm, wout_hbm, left_hbm, right_hbm, mom_hbm, lists_ref, count_ref,
    newmom_ref, search_in_ref, search_out_ref,
    x_ref, gl_ref, win_ref, wout_ref, mom_ref,
    wz, pg, slope, base, acc, acc_out, act_t, slope_next, acc_next, m_next,
    m_p, m_pc, m_q, m_rc, m_o,
    c_p, c_pc, c_q, c_rc, c_o,
    i_p, i_rc, i_q, i_ra, i_t, i_rb,
    o_p, o_rc, o_q, o_ra, o_t, o_rb,
    r_x, r_pk, r_rk, r_sum, r_rc, r_home,
    d_x, d_pk, d_rk,
    local, send, recv, z_near, z_far, z_recv, p_near, p_far, p_recv, n_send, n_recv, b_send, b_recv,
):
    s = lax.axis_index("section")
    dp = lax.axis_index("dp")
    c = lax.rem(dp, 2)
    y = lax.rem(dp // 2, 4)
    x = dp // 8
    last = sections - 1
    first_of = (x, y)
    second_of = (y, x)
    wide = s <= last - 9
    ids = {}

    def sid(key):
        return ids.setdefault(key, len(ids))

    def device(h, a, b):
        return (a * 4 + b) * 2 + c if h == 0 else (b * 4 + a) * 2 + c

    def remote(key, source, target, peer):
        number = sid(key)
        return pltpu.make_async_remote_copy(
            src_ref=source, dst_ref=target, send_sem=send.at[number], recv_sem=recv.at[number],
            device_id={"dp": peer}, device_id_type=MESH,
        )

    sibling = dp + 1 - 2 * c

    def peer_first(h, i):
        a = lax.rem(first_of[h] + i, 4)
        return a, device(h, a, second_of[h])

    def peer_second(h, i):
        b = lax.rem(second_of[h] + i, 4)
        return b, device(h, first_of[h], b)

    def go(copies):
        for copy in copies:
            copy.start()

    def land(copies):
        for copy in copies:
            copy.wait_recv()

    def sent(copies):
        for copy in copies:
            copy.wait_send()

    barrier = pltpu.get_barrier_semaphore()

    def greet(i, carry):
        pl.semaphore_signal(barrier, inc=1, device_id={"dp": lax.rem(dp + 2 * i, 32)}, device_id_type=MESH)
        return carry

    lax.fori_loop(1, 16, greet, 0)
    pl.semaphore_signal(barrier, inc=1, device_id={"dp": sibling}, device_id_type=MESH)
    below = lax.rem(s + last, sections)
    below_two = lax.rem(s + last - 1, sections)
    even = lax.rem(s, 2) == 0
    for peer in (below, below_two, lax.rem(s + 1, sections), lax.rem(s + 2, sections)):
        pl.semaphore_signal(barrier, inc=1, device_id={"section": peer}, device_id_type=MESH)

    fetches = {}

    def fetch(name, source, target):
        fetches[name] = pltpu.make_async_copy(source, target, local.at[len(fetches)])
        fetches[name].start()

    fetch("x", x_hbm, x_ref)
    fetch("win", win_hbm, win_ref)
    fetch("gl", gl_hbm, gl_ref)
    fetch("wout", wout_hbm, wout_ref)
    fetch("mom", mom_hbm, mom_ref)
    for h in range(2):
        rows = pl.ds(h * 64, 64)
        slots = pl.ds(first_of[h] * 4, 4)
        fetch(("left", h), left_hbm.at[:, rows], r_x.at[h, slots, 0])
        fetch(("right", h), right_hbm.at[:, rows], r_x.at[h, slots, 1])

    pl.semaphore_wait(barrier, 20)

    def to_section(source, target, send_sem, recv_sem, peer):
        return pltpu.make_async_remote_copy(
            src_ref=source, dst_ref=target, send_sem=send_sem, recv_sem=recv_sem,
            device_id={"section": peer}, device_id_type=MESH,
        )

    def slice_near(index):
        return to_section(wz.at[index], wz.at[index], z_near.at[index], z_recv.at[index], below)

    def slice_far(index):
        return to_section(wz.at[index], wz.at[index], z_far.at[index], z_recv.at[index], below_two)

    my_columns = pl.ds(pl.multiple_of(dp * 128, 128), 128)

    def own_near():
        return to_section(win_hbm.at[my_columns], wz.at[s], z_near.at[s], z_recv.at[s], below)

    def own_far():
        return to_section(win_hbm.at[my_columns], wz.at[s], z_far.at[s], z_recv.at[s], below_two)

    def pass_near(index):
        return to_section(pg.at[index], pg.at[index], p_near.at[index], p_recv.at[index], below)

    def pass_far(index):
        return to_section(pg.at[index], pg.at[index], p_far.at[index], p_recv.at[index], below_two)

    def share_state():
        return [
            to_section(base, acc_next, b_send.at[0], b_recv.at[0], below),
            to_section(slope, slope_next, b_send.at[1], b_recv.at[1], below),
        ]

    def places(k):
        if isinstance(k, int):
            return k // 8, k // 4 % 2, k % 4
        return k // 8, lax.rem(k // 4, 2), lax.rem(k, 4)

    def share_product(k):
        return to_section(m_o.at[places(k)], m_next.at[k], n_send.at[k], n_recv.at[k], below)

    def pair_product(k):
        return pltpu.make_async_remote_copy(
            src_ref=m_next.at[k], dst_ref=m_next.at[k], send_sem=n_send.at[k], recv_sem=n_recv.at[k],
            device_id={"dp": sibling}, device_id_type=MESH,
        )

    pl.when(s > 1)(lambda: own_far().start())
    pl.when(s > 0)(lambda: own_near().start())

    def roots_first():
        copies = []
        for h in range(2):
            mine = r_x.at[h, pl.ds(first_of[h] * 4, 4)]
            for i in range(1, 4):
                copies.append(remote(("ra", h, i), mine, mine, peer_first(h, i)[1]))
        return copies

    def roots_second():
        copies = []
        for h in range(2):
            for i in range(1, 4):
                b, peer = peer_second(h, i)
                copies.append(remote(("rb", h, i), r_pk.at[h, b], r_rk.at[h, i - 1], peer))
        return copies

    def roots_pair():
        return [remote(("rc",), r_sum.at[:, 1 - c], r_rc, sibling)]

    def roots_pack():
        land(roots_first())
        for h in range(2):
            def target(t, carry):
                b, core, kind = t // 4, lax.rem(t // 2, 2), lax.rem(t, 2)
                if h == 0:
                    place = (first_of[h] * 4 + b) * 2 + core
                else:
                    place = (b * 4 + first_of[h]) * 2 + core
                block = kind * 32 + place
                index = jnp.int32(0)
                found = jnp.int32(0)
                for a in range(4):
                    owner = device(h, a, second_of[h])
                    held = count_ref[0, owner]
                    for k in range(4):
                        hit = (lists_ref[0, k, owner] == block) & (held > k)
                        index = index + jnp.where(hit, a * 4 + k, 0)
                        found = found + jnp.where(hit, 1, 0)
                value = r_x[h, index]
                r_pk[h, b, core, kind] = jnp.where(found > 0, value, jnp.zeros_like(value))
                return carry
            lax.fori_loop(0, 16, target, 0)
        go(roots_second())

    fetches["x"].wait()
    fetches["win"].wait()
    pre = dot_nn(x_ref[...], win_ref[...])
    slope[...] = silu_slope(pre)
    act = jax.nn.silu(pre)
    act_t[...] = act.T.astype(BF16)
    fetches["gl"].wait()
    fetches["wout"].wait()
    base[...] = dot_nt(gl_ref[...], wout_ref[...])
    acc[...] = base[...]

    @pl.when(~even)
    def _():
        go(share_state())

    fetches["mom"].wait()
    for h in range(2):
        for k in range(4):
            r_x[h, first_of[h] * 4 + k, 2] = mom_ref[k, pl.ds(h * 64, 64)].astype(BF16)
        fetches[("left", h)].wait()
        fetches[("right", h)].wait()

    @pl.when(s <= SOON)
    def _():
        go(roots_first())

    wz[sections:] = jnp.zeros_like(wz[sections:])
    m_p[...] = jnp.zeros_like(m_p)
    c_p[...] = jnp.zeros_like(c_p)

    class Sum:
        def __init__(self, name, p, pc, q, rc, o):
            self.name, self.p, self.pc, self.q, self.rc, self.o = name, p, pc, q, rc, o

        def pair(self, stage, first, size):
            part = pl.ds(first, size)
            if stage == 0:
                return [remote((self.name, "pair", 0), self.p.at[part, :, :, :, 1 - c], self.pc.at[part], sibling)]
            mine = self.o.at[part, :, :, :, c]
            return [remote((self.name, "pair", 1), mine, mine, sibling)]

        def start(self, stage, first, size):
            number = sid((self.name, stage, first))
            part = pl.ds(first, size)
            if stage == 0:
                land(self.pair(0, first, size))
                for chunk in range(first, first + size):
                    for h in range(2):
                        both = self.p[chunk, h, :, :, c].astype(F32) + self.pc[chunk, h].astype(F32)
                        self.q[chunk, h] = both.astype(BF16)

            def one(i, carry):
                peer = lax.rem(dp + 2 * i, 32)
                if stage == 0:
                    source = self.q.at[part, :, peer // 8, lax.rem(peer // 2, 4)]
                    target = self.rc.at[i - 1, part]
                else:
                    source = target = self.o.at[part, :, x, y, c]
                pltpu.make_async_remote_copy(
                    src_ref=source, dst_ref=target, send_sem=send.at[number], recv_sem=recv.at[number],
                    device_id={"dp": peer}, device_id_type=MESH,
                ).start()
                return carry

            lax.fori_loop(1, 16, one, 0)

        def all_bytes(self, sems, stage, first, size):
            number = sid((self.name, stage, first))
            every = self.rc.at[:, pl.ds(first, size)]
            pltpu.make_async_copy(every, every, sems.at[number]).wait()

        def finish(self, stage, first, size):
            self.all_bytes(recv, stage, first, size)
            if stage == 0:
                part = pl.ds(first, size)
                total = self.q[part, :, x, y].astype(F32)
                for i in range(15):
                    total = total + self.rc[i, part].astype(F32)
                self.o[part, :, x, y, c] = total.astype(BF16)
            else:
                go(self.pair(1, first, size))
                land(self.pair(1, first, size))

        def drain(self, first, size):
            for stage in range(2):
                self.all_bytes(send, stage, first, size)
                sent(self.pair(stage, first, size))

    class Scatter:
        def __init__(self, name, p, rc, q, ra, t, rb):
            self.name, self.p, self.rc, self.q = name, p, rc, q
            self.ra, self.t, self.rb = ra, t, rb

        def fill(self, left, right_ref):
            def chip(n, carry):
                cx, cy = n // 4, lax.rem(n, 4)
                columns = pl.ds(pl.multiple_of(n * 256, 256), 256)
                product = dot_nn(left, right_ref[:, columns]).astype(BF16)
                for core in range(2):
                    block = product[:, core * 128:(core + 1) * 128]
                    self.p[0, cx, cy, core] = block[:64]
                    self.p[1, cy, cx, core] = block[64:]
                return carry
            lax.fori_loop(0, 16, chip, 0)

        def copies(self, stage):
            n = self.name
            if stage == 0:
                return [remote((n, 0), self.p.at[:, :, :, 1 - c], self.rc, sibling)]
            out = []
            for h in range(2):
                for i in range(1, 4):
                    if stage == 1:
                        a, peer = peer_first(h, i)
                        out.append(remote((n, 1, h, i), self.q.at[h, a], self.ra.at[h, i - 1], peer))
                    else:
                        b, peer = peer_second(h, i)
                        out.append(remote((n, 2, h, i), self.t.at[h, b], self.rb.at[h, i - 1], peer))
            return out

        def start(self, stage):
            go(self.copies(stage))

        def finish(self, stage):
            land(self.copies(stage))
            if stage == 0:
                for h in range(2):
                    for a in range(4):
                        self.q[h, a] = (self.p[h, a, :, c].astype(F32) + self.rc[h, a].astype(F32)).astype(BF16)
            elif stage == 1:
                for h in range(2):
                    total = self.q[h, first_of[h]].astype(F32)
                    for i in range(3):
                        total = total + self.ra[h, i].astype(F32)
                    self.t[h] = total.astype(BF16)

        def result(self):
            halves = []
            for h in range(2):
                total = self.t[h, second_of[h]].astype(F32)
                for i in range(3):
                    total = total + self.rb[h, i].astype(F32)
                halves.append(total)
            return jnp.concatenate(halves, axis=0)

        def drain(self):
            for stage in range(3):
                sent(self.copies(stage))

    m_sum = Sum("m", m_p, m_pc, m_q, m_rc, m_o)
    c_sum = Sum("c", c_p, c_pc, c_q, c_rc, c_o)
    into = Scatter("i", i_p, i_rc, i_q, i_ra, i_t, i_rb)
    outof = Scatter("o", o_p, o_rc, o_q, o_ra, o_t, o_rb)

    def product(t):
        block = dot_nn(wout_ref[:, my_columns], wz[s + t])
        m_p[places(t - 1)] = block.astype(BF16).reshape(4, 2, 16, 128)

    def relay(n, carry):
        odd = 2 * n + 1
        far = 2 * n + 2
        slice_far(s + far).wait_recv()

        @pl.when(s > 1)
        def _():
            slice_far(s + far).start()
            slice_near(s + far).start()

        pl.when(s == 1)(lambda: slice_near(s + far).start())
        slice_near(s + odd).wait_recv()
        product(odd)
        product(far)

        return carry

    steps = (last - s) // 2
    lax.fori_loop(0, steps, relay, 0)

    @pl.when(even)
    def _():
        slice_near(last).wait_recv()
        product(last - s)

    pl.when(wide)(lambda: go(m_sum.pair(0, 0, 2)))
    pl.when((~wide) & (s < last))(lambda: go(m_sum.pair(0, 0, 1)))
    pl.when(wide)(lambda: m_sum.start(0, 0, 2))
    pl.when((~wide) & (s < last))(lambda: m_sum.start(0, 0, 1))

    @pl.when(s <= EARLY)
    def _():
        outof.fill(act_t[...], gl_ref)
        outof.start(0)

    @pl.when(wide)
    def _():
        m_sum.finish(0, 0, 2)
        m_sum.start(1, 0, 2)

    @pl.when(s <= EARLY)
    def _():
        outof.finish(0)
        roots_pack()
        outof.start(1)

    pl.when(wide)(lambda: m_sum.finish(1, 0, 2))

    @pl.when((~wide) & (s < last))
    def _():
        m_sum.finish(0, 0, 1)
        m_sum.start(1, 0, 1)
        m_sum.finish(1, 0, 1)

    @pl.when(~even)
    def _():
        def give(n, carry):
            share_product(last - 1 - s - 2 * n - (1 - c)).start()
            return carry
        lax.fori_loop(0, (last - s) // 2, give, 0)

    pl.when(s > SOON)(lambda: go(roots_first()))

    def cross(index):
        c_p[places(index - s - 1)] = dot_nn(act_t[...], pg[index]).astype(BF16).reshape(4, 2, 16, 128)

    def own_term(index):
        return dot_nt(pg[index], m_o[places(index - s - 1)].reshape(128, 128))

    def next_term(index):
        return dot_nt(pg[index], m_next[index - s - 2].reshape(128, 128))

    lowest = (s + 2) // 2

    @pl.when(even)
    def _():
        land(share_state())

        def come(high, low):
            pass_far(high).wait_recv()
            pass_far(low).wait_recv()

            @pl.when(s > 0)
            def _():
                pass_far(high).start()
                pass_far(low).start()

        def products(high, low):
            share_product(high - s - 2 - c).wait_recv()

        def collect(n, carry):
            high, low = 15 - 2 * n, 14 - 2 * n
            come(high, low)

            @pl.when(s > 0)
            def _():
                pass_near(high).start()
                pass_near(low).start()
            return carry

        def add(n, carry):
            high, low = 15 - 2 * n, 14 - 2 * n
            products(high, low)
            acc_next[...] += next_term(high) + next_term(low)
            acc[...] += own_term(high) + own_term(low)
            return carry

        def spread(n, carry):
            k = last - 2 - s - 2 * n - (1 - c)
            share_product(k).wait_recv()
            pair_product(k).start()
            return carry

        lax.fori_loop(0, 7 - lowest, collect, 0)
        lax.fori_loop(0, 8 - lowest, spread, 0)
        lax.fori_loop(0, 7 - lowest, add, 0)

        @pl.when(s < last - 1)
        def _():
            high, low = 2 * lowest + 1, 2 * lowest
            products(high, low)
            come(high, low)
            pg[s + 1] = ((acc_next[...] + next_term(high) + next_term(low)) * slope_next[...]).astype(BF16)
            pl.when(s > 0)(lambda: pass_far(s + 1).start())
            pg[s] = ((acc[...] + own_term(high) + own_term(low) + own_term(s + 1)) * slope[...]).astype(BF16)

            @pl.when(s > 0)
            def _():
                pass_far(s).start()
                for index in (high, low, s + 1, s):
                    pass_near(index).start()

        @pl.when(s == last - 1)
        def _():
            pg[s + 1] = (acc_next[...] * slope_next[...]).astype(BF16)
            pass_far(s + 1).start()
            pg[s] = ((acc[...] + own_term(s + 1)) * slope[...]).astype(BF16)
            pass_far(s).start()
            pass_near(s + 1).start()
            pass_near(s).start()

    @pl.when(~even)
    def _():
        def collect(n, carry):
            high, low = 15 - 2 * n, 14 - 2 * n
            pass_far(high).wait_recv()
            pass_far(low).wait_recv()
            acc[...] += own_term(high) + own_term(low)
            return carry

        lax.fori_loop(0, 8 - lowest, collect, 0)
        pg[s] = (acc[...] * slope[...]).astype(BF16)

    def cross_two(n, carry):
        cross(s + 1 + 2 * n)
        cross(s + 2 + 2 * n)
        return carry

    lax.fori_loop(0, (last - s) // 2, cross_two, 0)
    pl.when(even)(lambda: cross(last))
    pl.when(wide)(lambda: go(c_sum.pair(0, 0, 2)))
    pl.when((~wide) & (s < last))(lambda: go(c_sum.pair(0, 0, 1)))

    into.fill(pg[s].astype(F32).T.astype(BF16), x_ref)
    into.start(0)
    pl.when(wide)(lambda: c_sum.start(0, 0, 2))
    pl.when((~wide) & (s < last))(lambda: c_sum.start(0, 0, 1))

    into.finish(0)
    into.start(1)

    @pl.when(wide)
    def _():
        c_sum.finish(0, 0, 2)
        c_sum.start(1, 0, 2)

    @pl.when((~wide) & (s < last))
    def _():
        c_sum.finish(0, 0, 1)
        c_sum.start(1, 0, 1)

    @pl.when(s > EARLY)
    def _():
        roots_pack()
        outof.fill(act_t[...], gl_ref)
        outof.start(0)
        outof.finish(0)
        outof.start(1)

    outof.finish(1)
    outof.start(2)
    into.finish(1)
    into.start(2)

    land(roots_second())
    for h in range(2):
        total = r_pk[h, second_of[h]].astype(F32)
        for i in range(3):
            total = total + r_rk[h, i].astype(F32)
        r_sum[h] = total.astype(BF16)
    go(roots_pair())

    def terms(first):
        total = acc_out[...]
        for k in range(first, first + 8):
            total = total + dot_nt(c_o[places(k)].reshape(128, 128), wz[s + 1 + k])
        acc_out[...] = total

    outof.finish(2)
    acc_out[...] = outof.result()

    into.finish(2)
    land(roots_pair())
    for h in range(2):
        merged = (r_sum[h, c].astype(F32) + r_rc[h].astype(F32)).astype(BF16)
        for kind in range(2):
            for what in range(3):
                r_home[kind, what, pl.ds(h * 64, 64)] = merged[kind, what]

    def direct(kind, grad32, out_ref):
        grad = grad32.astype(BF16)
        exact = grad.astype(F32)
        first = dot_nn(r_home[kind, 0], grad)
        high = first.astype(BF16)
        low = (first - high.astype(F32)).astype(BF16)
        right = r_home[kind, 1]
        precond = dot_nn(high, right) + dot_nn(low, right)
        grad_sq = jnp.sum(jnp.sum(exact * exact, axis=1, keepdims=True), axis=0, keepdims=True)
        pre_sq = jnp.sum(jnp.sum(precond * precond, axis=1, keepdims=True), axis=0, keepdims=True)
        direction = precond * (jnp.sqrt(grad_sq) * lax.rsqrt(pre_sq + 1e-06))
        out_ref[...] = (MOMENTUM_DECAY * r_home[kind, 2].astype(F32) + direction).astype(BF16)
        rounded = direction.astype(BF16)
        for h in range(2):
            d_x[h, first_of[h], c, kind] = rounded[h * 64:(h + 1) * 64]

    direct(0, into.result().T * (1.0 / 32), search_in_ref)

    def way_first(kind):
        copies = []
        for h in range(2):
            mine = d_x.at[h, first_of[h], c, kind]
            for i in range(1, 4):
                copies.append(remote(("da", h, i, kind), mine, mine, peer_first(h, i)[1]))
        return copies

    go(way_first(0))

    @pl.when(wide)
    def _():
        c_sum.finish(1, 0, 2)
        terms(8)
        terms(0)

    @pl.when((~wide) & (s < last))
    def _():
        c_sum.finish(1, 0, 1)
        terms(0)

    direct(1, acc_out[...] * (1.0 / 32), search_out_ref)

    def way_pair():
        mine = d_x.at[:, :, c]
        return [remote(("dc",), mine, mine, sibling)]

    def way_second():
        copies = []
        for h in range(2):
            for i in range(1, 4):
                b, peer = peer_second(h, i)
                copies.append(remote(("db", h, i), d_pk.at[h, b], d_rk.at[h, i - 1], peer))
        return copies

    go(way_first(1))
    land(way_first(0))
    land(way_first(1))
    go(way_pair())
    land(way_pair())
    for h in range(2):
        def slot(t, carry):
            b, k = t // 4, lax.rem(t, 4)
            owner = device(h, first_of[h], b)
            block = lists_ref[0, k, owner]
            kind = block // 32
            hx, hy, core = lax.rem(block // 8, 4), lax.rem(block // 2, 4), lax.rem(block, 2)
            a, row = (hx, hy) if h == 0 else (hy, hx)
            here = (row == second_of[h]) & (count_ref[0, owner] > k)
            value = d_x[h, a, core, kind]
            d_pk[h, b, k] = jnp.where(here, value, jnp.zeros_like(value))
            return carry
        lax.fori_loop(0, 16, slot, 0)
    go(way_second())
    land(way_second())
    for h in range(2):
        total = d_pk[h, second_of[h]].astype(F32)
        for i in range(3):
            total = total + d_rk[h, i].astype(F32)
        rows = pl.ds(h * 64, 64)
        for k in range(4):
            old = mom_ref[k, rows]
            new = MOMENTUM_DECAY * old + total[k]
            newmom_ref[k, rows] = jnp.where(count_ref[0, dp] > k, new, old)

    pl.when(s > 1)(lambda: own_far().wait_send())
    pl.when(s > 0)(lambda: own_near().wait_send())

    def leave(t, carry):
        @pl.when(lax.rem(t, 2) == 0)
        def _():
            pl.when(s > 1)(lambda: slice_far(s + t).wait_send())
            pl.when(s > 0)(lambda: slice_near(s + t).wait_send())
        return carry

    lax.fori_loop(1, sections - s, leave, 0)

    @pl.when(even & (s > 0))
    def _():
        def passed(index, carry):
            pass_far(index).wait_send()
            pass_near(index).wait_send()
            return carry
        lax.fori_loop(s, sections, passed, 0)

    @pl.when(~even)
    def _():
        sent(share_state())

        def given(n, carry):
            share_product(last - 1 - s - 2 * n - (1 - c)).wait_send()
            return carry
        lax.fori_loop(0, (last - s) // 2, given, 0)

    @pl.when(even)
    def _():
        def given_pair(n, carry):
            pair_product(last - 2 - s - 2 * n - (1 - c)).wait_send()
            return carry
        lax.fori_loop(0, 8 - lowest, given_pair, 0)

    @pl.when(wide)
    def _():
        m_sum.drain(0, 2)
        c_sum.drain(0, 2)

    @pl.when((~wide) & (s < last))
    def _():
        m_sum.drain(0, 1)
        c_sum.drain(0, 1)

    into.drain()
    outof.drain()
    sent(roots_first())
    sent(roots_second())
    sent(roots_pair())
    sent(way_first(0))
    sent(way_first(1))
    sent(way_pair())
    sent(way_second())


def on_device(
    sections, saved_inputs, loss_grad, w_in, w_out, left_root, right_root, momentum, owned_blocks, owned_count
):
    vmem = pl.BlockSpec(memory_space=pltpu.VMEM)
    hbm = pl.BlockSpec(memory_space=pltpu.HBM)
    smem = pl.BlockSpec(memory_space=pltpu.SMEM)

    def room(*shape, kind=BF16):
        return pltpu.VMEM(shape, kind)

    def sum_room():
        return [
            room(2, 2, 4, 4, 2, 16, 128), room(2, 2, 4, 4, 16, 128), room(2, 2, 4, 4, 16, 128), room(15, 2, 2, 16, 128), room(2, 2, 4, 4, 2, 16, 128),
        ]

    def scatter_room():
        return [
            room(2, 4, 4, 2, 64, 128), room(2, 4, 4, 64, 128), room(2, 4, 4, 64, 128),
            room(2, 3, 4, 64, 128), room(2, 4, 64, 128), room(2, 3, 64, 128),
        ]

    scratch = (
        [
            room(128, 4096), room(128, 4096), room(4096, 128), room(128, 4096), room(4, 128, 128, kind=F32),
            room(sections + 8, 128, 128), room(sections, 128, 128),
            room(128, 128, kind=F32), room(128, 128, kind=F32), room(128, 128, kind=F32), room(128, 128, kind=F32), room(128, 128),
            room(128, 128, kind=F32), room(128, 128, kind=F32), room(16, 4, 2, 16, 128),
        ]
        + sum_room() + sum_room() + scatter_room() + scatter_room()
        + [
            room(2, 16, 3, 64, 128), room(2, 4, 2, 2, 3, 64, 128), room(2, 3, 2, 2, 3, 64, 128),
            room(2, 2, 2, 3, 64, 128), room(2, 2, 3, 64, 128), room(2, 3, 128, 128),
            room(2, 4, 2, 2, 64, 128), room(2, 4, 4, 64, 128), room(2, 3, 4, 64, 128),
        ]
        + [pltpu.SemaphoreType.DMA((9,))]
        + [pltpu.SemaphoreType.DMA((COPIES,))] * 2
        + [pltpu.SemaphoreType.DMA((sections,))] * 8
        + [pltpu.SemaphoreType.DMA((2,))] * 2
    )
    new_mom, search_in, search_out = pl.pallas_call(
        functools.partial(kernel, sections),
        out_shape=(
            jax.ShapeDtypeStruct((4, 128, 128), F32),
            jax.ShapeDtypeStruct((128, 128), BF16),
            jax.ShapeDtypeStruct((128, 128), BF16),
        ),
        in_specs=[hbm] * 7 + [smem] * 2,
        out_specs=(vmem, vmem, vmem),
        scratch_shapes=scratch,
        compiler_params=pltpu.CompilerParams(
            collective_id=0, has_side_effects=True, vmem_limit_bytes=60 * 1024 * 1024
        ),
        name="drain",
    )(
        saved_inputs.reshape(128, 4096), loss_grad.reshape(128, 4096), w_in[0], w_out[0],
        left_root[0, 0], right_root[0, 0], momentum[0, 0],
        jnp.swapaxes(owned_blocks, 1, 2), owned_count,
    )
    return new_mom[None, None], search_in[None], search_out[None]


def solution(mesh):
    placed = (
        P("section", None, "dp", None),
        P(None, "dp", None),
        P("section", None, None),
        P("section", None, None),
        P("section", "dp", None, None, None),
        P("section", "dp", None, None, None),
        P("section", "dp", None, None, None),
        P("section", None, None),
        P("section", None),
    )
    return jax.shard_map(
        functools.partial(on_device, mesh.shape["section"]),
        mesh=mesh,
        in_specs=placed,
        out_specs=(
            P("section", "dp", None, None, None),
            P("section", "dp", None),
            P("section", None, "dp"),
        ),
        check_vma=False,
    )
```
